256 devices in a mesh: wide: 64 (over y, z, core), grp: 4 (over x).
Axes of the slice: x: 4, y: 4, z: 8, core: 2. Of those that a mesh axis runs over, the one named last changes fastest.
Arguments:
- slab: float32 [512, 4, 128, 128], P(None, 'grp', 'wide'), may hold values from -400 to 400
- hblocks: float32 [4, 128, 5, 128, 128], P('grp', 'wide'), may hold values from -0.25 to 0.25
- blist: int32 [4, 128, 5], P('grp', 'wide'), may hold values from 0 to 8, as said below
- rotation: float32 [64, 8, 8], replicated, may hold values from -2 to 2
Outputs:
- rotated: float32 [512, 4, 128, 128], P('wide', 'grp')
The draws below stay inside these ranges and needn't reach their ends.
Inputs may be any that keep to these rules, and one draw needn't show every extreme that they name: `blist`: entry 0 of every row block's list is 4 (the block itself); the other entries are distinct codes other than 4.
All inputs are finite; a program needn't handle non-finite values.
Results may differ from the reference program's by a relative error of at most 0.00012.
Values sent between devices are 32-bit elements; how exact they have to be, the bound alone decides.
A program may use at most 64 MiB of HBM per device.

```python
import jax
import jax.numpy as jnp
from jax import lax

VEC = 8
BS = 128
K = 5
DEG = 4
S = 512
SBLK = 64
GRPS = 4
QBLK = 128
NODES = 65536


def draw_blist(key, part):
    key = jax.random.fold_in(key, 7)
    scores = jax.random.randint(key, (GRPS, QBLK, 8), 0, 1 << 20, dtype=jnp.int32)
    scores = scores * 8 + jnp.arange(8, dtype=jnp.int32)
    ordering = jnp.argsort(scores, axis=-1).astype(jnp.int32)
    neighbours = ordering + (ordering >= 4).astype(jnp.int32)
    self_code = jnp.full((GRPS, QBLK, 1), 4, jnp.int32)
    return jnp.concatenate([self_code, neighbours[:, :, :K - 1]], axis=-1)


def draw_slab(key, part):
    key = jax.random.fold_in(key, 11)
    key_list = jax.random.split(key, 3)
    rising = 3.0 ** (jnp.arange(QBLK, dtype=jnp.float32) / max(QBLK - 1, 1))
    block_scale = 10.0 ** jax.random.uniform(key_list[1], (1, GRPS, QBLK, 1), jnp.float32)
    state_scale = 10.0 ** jax.random.uniform(key_list[2], (S, 1, 1, 1), jnp.float32)
    basic_values = jnp.clip(jax.random.normal(key_list[0], (S, GRPS, QBLK, BS), jnp.float32), -6.0, 6.0)
    return basic_values * rising[None, None, :, None] * block_scale * state_scale / 10.0


def shard_levels(stream_key, dims, shards, least, high):
    def one(position, parts):
        heights = jax.random.uniform(jax.random.fold_in(jax.random.fold_in(stream_key, 6), position), (parts,), jnp.float32, least / len(shards), high / len(shards))
        return jnp.repeat(jnp.exp(heights), dims[position] // parts).reshape((-1,) + (1,) * (len(dims) - position - 1))

    gain = one(*shards[0])
    for cut in shards[1:]:
        gain = gain * one(*cut)
    return gain


def gaussian(rng, dims, deviation, reach, pieces=(), kind=jnp.bfloat16):
    factor_of = shard_levels(rng, dims, pieces, -0.22, 0.18) if pieces else 1.0
    entries = jax.random.normal(rng, dims, jnp.float32) * deviation * factor_of
    return jnp.minimum(jnp.maximum(entries, -reach), reach).astype(kind)


def setup_inputs(seed: int = 0) -> dict:
    key_of = jax.random.split(jax.random.key(seed), 5)
    return {
        "slab": draw_slab(jax.random.fold_in(key_of[4], 71), 0),
        "hblocks": gaussian(key_of[1], (GRPS, QBLK, K, BS, BS), (K * BS) ** -0.5, 0.25, ((0, 4), (1, 64)), jnp.float32),
        "blist": draw_blist(jax.random.fold_in(key_of[4], 71), 0),
        "rotation": gaussian(key_of[3], (SBLK, VEC, VEC), VEC ** -0.5, 2.0, (), jnp.float32),
    }


def apply_operator(field_in, hblocks, blist):
    padded = jnp.pad(field_in, ((0, 0), (1, 1), (1, 1), (0, 0)))
    grp_rows = jnp.arange(field_in.shape[1], dtype=jnp.int32)[:, None]
    blk_cols = jnp.arange(field_in.shape[2], dtype=jnp.int32)[None, :]
    summed = jnp.zeros(field_in.shape, jnp.float32)
    for slot_index in range(blist.shape[2]):
        block_code = blist[:, :, slot_index]
        picked = padded[:, grp_rows + block_code // 3, blk_cols + block_code % 3]
        summed = summed + jnp.einsum('gqij,sgqj->sgqi', hblocks[:, :, slot_index], picked, precision=lax.Precision.HIGHEST)
    return summed

def mixing(gram_mat, rotation):
    lower = jnp.linalg.cholesky(gram_mat)
    return lax.linalg.triangular_solve(lower, jnp.swapaxes(rotation, -1, -2), left_side=False, lower=True)

def reference(slab, hblocks, blist, rotation):
    previous = slab
    current = apply_operator(slab, hblocks, blist)
    for degree_step in range(DEG - 1):
        following = 2.0 * apply_operator(current, hblocks, blist) - previous
        previous, current = (current, following)
    state_blocks = current.reshape(SBLK, VEC, -1)
    gram_mat = jnp.einsum('bam,bcm->bac', state_blocks, state_blocks, precision=lax.Precision.HIGHEST) / NODES
    mixer = mixing(gram_mat, rotation)
    rotated = jnp.einsum('bad,bdm->bam', mixer, state_blocks, precision=lax.Precision.HIGHEST)
    return rotated.reshape(current.shape)
```

```python
import functools

import jax
import jax.numpy as jnp
from jax import lax
from jax.experimental import pallas as pl
from jax.experimental.pallas import tpu as pltpu
from jax.sharding import PartitionSpec as P

MESH = pl.DeviceIdType.MESH
F32 = jnp.float32
BF16 = jnp.bfloat16
VEC = 8
DEG = 4
BS = 128
K = 5
G = 4
PAIRS = [(a, c) for a in range(VEC) for c in range(a + 1)]
PAIR_ROWS = 40


def split(value):
    high = value.astype(BF16)
    low = (value - high.astype(F32)).astype(BF16)
    return high, low


def kernel(
    wide,
    nodes,
    slab,
    hblocks,
    codes,
    rotation,
    out,
    slab_in,
    h_in,
    codes_in,
    codes_sm,
    hs,
    fields,
    halo,
    xs,
    fin,
    recv,
    gram,
    rot_in,
    rot_wide,
    mixer,
    local_sem,
    slab_send,
    slab_recv,
    codes_send,
    codes_recv,
    h_send,
    h_recv,
    halo_send,
    halo_recv,
    fin_send,
    fin_recv,
    gram_send,
    gram_recv,
):
    w = lax.axis_index("wide")
    g = lax.axis_index("grp")
    nb = wide // G
    chunk = VEC * nb
    source = w // nb
    is_own = source == g
    has_left = w > 0
    has_right = w < wide - 1

    def remote(src, dst, send_sem, recv_sem, to):
        return pltpu.make_async_remote_copy(
            src_ref=src, dst_ref=dst, send_sem=send_sem, recv_sem=recv_sem, device_id=to, device_id_type=MESH
        )

    def arrived(ref, sem):
        pltpu.make_async_copy(ref, ref, sem).wait()

    def row_at(d):
        return lax.rem(g + d, G)

    barrier = pltpu.get_barrier_semaphore()
    for d in range(1, G):
        pl.semaphore_signal(barrier, inc=1, device_id=(w, row_at(d)), device_id_type=MESH)

    @pl.when(has_left)
    def _():
        pl.semaphore_signal(barrier, inc=1, device_id=(w - 1, g), device_id_type=MESH)

    @pl.when(has_right)
    def _():
        pl.semaphore_signal(barrier, inc=1, device_id=(w + 1, g), device_id_type=MESH)

    @pl.loop(0, wide)
    def _(i):
        @pl.when(jnp.logical_not(jnp.logical_and(i == w, is_own)))
        def _():
            pl.semaphore_signal(barrier, inc=1, device_id=(i, source), device_id_type=MESH)

    own_slab = pltpu.make_async_copy(slab.at[pl.ds(g * 2 * chunk, 2 * chunk)], slab_in.at[g], local_sem.at[0])
    own_slab.start()
    own_h = pltpu.make_async_copy(hblocks, h_in.at[g], local_sem.at[1])
    own_h.start()
    own_codes = pltpu.make_async_copy(codes, codes_in.at[g], local_sem.at[2])
    own_codes.start()
    own_rot = pltpu.make_async_copy(rotation.at[w], rot_in, local_sem.at[3])
    own_rot.start()

    zero = jnp.zeros((2 * chunk, BS), BF16)
    for parity in range(2):
        for col in range(4):
            xs[parity, col] = zero
            xs[parity, 20 + col] = zero

        @pl.when(jnp.logical_not(has_left))
        def _():
            for r in range(G):
                xs[parity, (r + 1) * 4] = zero

        @pl.when(jnp.logical_not(has_right))
        def _():
            for r in range(G):
                xs[parity, (r + 1) * 4 + 3] = zero

    peers = G - 1 + wide - is_own.astype(jnp.int32) + has_left.astype(jnp.int32) + has_right.astype(jnp.int32)
    pl.semaphore_wait(barrier, peers)

    def slab_copy(d):
        to = row_at(d)
        return remote(
            slab.at[pl.ds(to * 2 * chunk, 2 * chunk)], slab_in.at[g], slab_send.at[d], slab_recv.at[g], (w, to)
        )

    def codes_copy(d):
        return remote(codes, codes_in.at[g], codes_send.at[d], codes_recv.at[g], (w, row_at(d)))

    def h_copy(half, d):
        return remote(
            hblocks.at[half], h_in.at[g, half], h_send.at[half, d // 2], h_recv.at[g, half], (w, row_at(d))
        )

    def h_forward(half, d):
        origin = row_at(G - d)
        return remote(
            h_in.at[origin, half], h_in.at[origin, half], h_send.at[half, 2], h_recv.at[origin, half], (w, row_at(d))
        )

    for d in (1, 3, 2):
        slab_copy(d).start()
    for d in (1, 3, 2):
        codes_copy(d).start()
    h_copy(0, 1).start()
    h_copy(1, 3).start()
    h_copy(1, 1).start()
    h_copy(0, 3).start()

    def split_h(r):
        @pl.loop(0, 2)
        def _(q):
            for k in range(K):
                high, low = split(h_in[r, q, k])
                hs[r, q, 0:BS, k * BS : (k + 1) * BS] = high
                hs[r, q, BS : 2 * BS, k * BS : (k + 1) * BS] = low

    def store_split(parity, position, value):
        high, low = split(value)
        xs[parity, position, 0:chunk] = high
        xs[parity, position, chunk : 2 * chunk] = low

    def halo_copy(n, r, side):
        to = w - 1 if side == 0 else w + 1
        return remote(
            fields.at[n, r, side],
            halo.at[n, r, 1 - side],
            halo_send.at[n, r, side],
            halo_recv.at[n, r, 1 - side],
            (to, g),
        )

    def send_halos(n, r):
        @pl.when(has_left)
        def _():
            halo_copy(n, r, 0).start()

        @pl.when(has_right)
        def _():
            halo_copy(n, r, 1).start()

    def take_halos(n):
        parity = n % 2

        @pl.loop(0, G)
        def _(r):
            @pl.when(has_left)
            def _():
                halo_copy(n, r, 1).wait_recv()
                store_split(parity, (r + 1) * 4, halo[n, r, 0])

            @pl.when(has_right)
            def _():
                halo_copy(n, r, 0).wait_recv()
                store_split(parity, (r + 1) * 4 + 3, halo[n, r, 1])

    def product(n, r, q):
        parity = n % 2
        picked = [xs[parity, r * 4 + q + codes_sm[r, q, k]] for k in range(K)]
        both = jnp.concatenate(picked, axis=1)
        p = lax.dot_general(both, hs[r, q], (((1,), (1,)), ((), ())), preferred_element_type=F32)
        small = p[:chunk, BS:] + p[chunk:, :BS] + p[chunk:, BS:]
        return p[:chunk, :BS] + small

    def apply_row(n, r):
        for q in range(2):
            value = product(n, r, q)
            if n > 0:
                value = 2.0 * value - fields[n - 1, r, q]
            if n + 1 < DEG:
                fields[n + 1, r, q] = value
                store_split((n + 1) % 2, (r + 1) * 4 + 1 + q, value)
            else:
                fin[r, :, q * VEC : (q + 1) * VEC, :] = value.reshape(nb, VEC, BS)
        if n + 1 < DEG:
            send_halos(n + 1, r)

    own_h.wait()
    split_h(g)
    own_rot.wait()
    rot = rot_in[...]
    for c in range(VEC):
        for a in range(VEC):
            rot_wide[c * VEC + a] = jnp.broadcast_to(rot[c : c + 1, a : a + 1], (VEC, BS))

    def start_row(r):
        for q in range(2):
            value = slab_in[r, pl.ds(q, chunk, stride=2), :]
            fields[0, r, q] = value
            store_split(0, (r + 1) * 4 + 1 + q, value)
        send_halos(0, r)

    own_slab.wait()
    start_row(g)
    for d in (1, 3, 2):
        arrived(slab_in.at[row_at(d)], slab_recv.at[row_at(d)])
        start_row(row_at(d))

    own_codes.wait()
    for d in (1, 3, 2):
        arrived(codes_in.at[row_at(d)], codes_recv.at[row_at(d)])
    to_scalars = pltpu.make_async_copy(codes_in, codes_sm, local_sem.at[4])
    to_scalars.start()
    to_scalars.wait()

    def h_wait(d, half):
        r = row_at(d)
        arrived(h_in.at[r, half], h_recv.at[r, half])

    take_halos(0)
    apply_row(0, g)
    h_wait(3, 0)
    h_forward(0, 1).start()
    h_wait(1, 1)
    h_forward(1, 3).start()
    h_wait(3, 1)
    split_h(row_at(3))
    apply_row(0, row_at(3))
    h_wait(1, 0)
    split_h(row_at(1))
    apply_row(0, row_at(1))
    h_wait(2, 0)
    h_wait(2, 1)
    split_h(row_at(2))
    apply_row(0, row_at(2))

    for n in range(1, DEG - 1):
        take_halos(n)

        @pl.loop(0, G)
        def _(r):
            apply_row(n, r)

    take_halos(DEG - 1)

    @pl.loop(0, G)
    def _(d):
        r = row_at(d)
        apply_row(DEG - 1, r)

        @pl.loop(0, nb)
        def _(i):
            b = lax.rem(i + w, nb)
            to = g * nb + b
            own = jnp.logical_and(to == w, r == g)

            @pl.when(jnp.logical_not(own))
            def _():
                remote(
                    fin.at[r, b], recv.at[pl.ds(w * 2 * VEC, 2 * VEC)], fin_send.at[0], fin_recv.at[0], (to, r)
                ).start()

            @pl.when(own)
            def _():
                pltpu.make_async_copy(
                    fin.at[r, b], recv.at[pl.ds(w * 2 * VEC, 2 * VEC)], fin_recv.at[0]
                ).start()

    arrived(recv, fin_recv.at[0])

    groups = 2 * wide // VEC

    def tiles(group):
        return [recv[pl.ds(group * VEC * VEC + s, VEC, stride=VEC), :] for s in range(VEC)]

    def add(group, sums):
        x = tiles(group)
        return tuple(total + x[a] * x[c] for total, (a, c) in zip(sums, PAIRS))

    sums = lax.fori_loop(0, groups, add, tuple(jnp.zeros((VEC, BS), F32) for _ in PAIRS))
    for i, total in enumerate(sums):
        gram[g, i : i + 1, :] = jnp.sum(total, axis=0, keepdims=True)
    for i in range(len(PAIRS), PAIR_ROWS):
        gram[g, i : i + 1, :] = jnp.zeros((1, BS), F32)

    def gram_copy(d):
        return remote(gram.at[g], gram.at[g], gram_send.at[d], gram_recv.at[g], (w, row_at(d)))

    for d in (1, 3, 2):
        gram_copy(d).start()
    for d in (1, 3, 2):
        arrived(gram.at[row_at(d)], gram_recv.at[row_at(d)])
    whole = (gram[0] + gram[1]) + (gram[2] + gram[3])
    whole = jnp.sum(whole, axis=1, keepdims=True) * (1.0 / nodes)
    entry = {pair: jnp.broadcast_to(whole[i : i + 1, :], (VEC, BS)) for i, pair in enumerate(PAIRS)}
    lower, inverse = {}, []
    for j in range(VEC):
        rest = entry[j, j]
        for k in range(j):
            rest = rest - lower[j, k] * lower[j, k]
        root = lax.rsqrt(rest)
        root = root * (1.5 - 0.5 * rest * root * root)
        inverse.append(root)
        for i in range(j + 1, VEC):
            value = entry[i, j]
            for k in range(j):
                value = value - lower[i, k] * lower[j, k]
            lower[i, j] = value * root
    for a in range(VEC):
        row = {}
        for c in reversed(range(VEC)):
            value = rot_wide[c * VEC + a]
            for k in range(c + 1, VEC):
                value = value - row[k] * lower[k, c]
            row[c] = value * inverse[c]
            mixer[a * VEC + c] = row[c]

    @pl.loop(0, groups)
    def _(group):
        x = tiles(group)
        for a in range(VEC):
            value = mixer[a * VEC] * x[0]
            for c in range(1, VEC):
                value = value + mixer[a * VEC + c] * x[c]
            out[a, 0, pl.ds(pl.multiple_of(group * VEC, VEC), VEC), :] = value

    for d in range(1, G):
        slab_copy(d).wait_send()
        codes_copy(d).wait_send()
        gram_copy(d).wait_send()
    for half in range(2):
        h_copy(half, 1).wait_send()
        h_copy(half, 3).wait_send()
    h_forward(0, 1).wait_send()
    h_forward(1, 3).wait_send()

    @pl.loop(0, DEG)
    def _(n):
        @pl.loop(0, G)
        def _(r):
            @pl.when(has_left)
            def _():
                halo_copy(n, r, 0).wait_send()

            @pl.when(has_right)
            def _():
                halo_copy(n, r, 1).wait_send()

    @pl.when(is_own)
    def _():
        part = recv.at[pl.ds(0, (wide - 1) * 2 * VEC)]
        pltpu.make_async_copy(part, part, fin_send.at[0]).wait()

    @pl.when(jnp.logical_not(is_own))
    def _():
        pltpu.make_async_copy(recv, recv, fin_send.at[0]).wait()


def body(slab, hblocks, blist, rotation):
    wide = lax.axis_size("wide")
    states = slab.shape[0]
    chunk = states // G
    nb = wide // G
    nodes = G * 2 * wide * BS
    offsets = (blist // 3) * 4 + blist % 3
    codes = jnp.pad(offsets.reshape(2, K), ((0, 6), (0, BS - K)))
    dma = pltpu.SemaphoreType.DMA
    any_space = pl.BlockSpec(memory_space=pl.ANY)
    return pl.pallas_call(
        functools.partial(kernel, wide, nodes),
        out_shape=jax.ShapeDtypeStruct((VEC, 1, 2 * wide, BS), F32),
        in_specs=[any_space, any_space, any_space, any_space],
        out_specs=pl.BlockSpec(memory_space=pltpu.VMEM),
        scratch_shapes=[
            pltpu.VMEM((G, 2 * chunk, BS), F32),
            pltpu.VMEM((G, 2, K, BS, BS), F32),
            pltpu.VMEM((G, 8, BS), jnp.int32),
            pltpu.SMEM((G, 8, BS), jnp.int32),
            pltpu.VMEM((G, 2, 2 * BS, K * BS), BF16),
            pltpu.VMEM((DEG, G, 2, chunk, BS), F32),
            pltpu.VMEM((DEG, G, 2, chunk, BS), F32),
            pltpu.VMEM((2, 24, 2 * chunk, BS), BF16),
            pltpu.VMEM((G, nb, 2 * VEC, BS), F32),
            pltpu.VMEM((wide * 2 * VEC, BS), F32),
            pltpu.VMEM((G, PAIR_ROWS, BS), F32),
            pltpu.VMEM((VEC, VEC), F32),
            pltpu.VMEM((VEC * VEC, VEC, BS), F32),
            pltpu.VMEM((VEC * VEC, VEC, BS), F32),
            dma((5,)),
            dma((G,)),
            dma((G,)),
            dma((G,)),
            dma((G,)),
            dma((2, 3)),
            dma((G, 2)),
            dma((DEG, G, 2)),
            dma((DEG, G, 2)),
            dma((1,)),
            dma((1,)),
            dma((G,)),
            dma((G,)),
        ],
        compiler_params=pltpu.CompilerParams(
            collective_id=0, has_side_effects=True, vmem_limit_bytes=40 * 1024 * 1024
        ),
        cost_estimate=pl.CostEstimate(flops=3 * 10**9, bytes_accessed=2 * 1024 * 1024, transcendentals=0),
    )(slab.reshape(2 * states, BS), hblocks.reshape(2, K, BS, BS), codes, rotation)


def solution(mesh):
    in_specs = (
        P(None, "grp", "wide", None),
        P("grp", "wide", None, None, None),
        P("grp", "wide", None),
        P(),
    )
    out_specs = P("wide", "grp", None, None)
    return jax.shard_map(body, mesh=mesh, in_specs=in_specs, out_specs=out_specs, check_vma=False)
```

```python
import functools

import jax
import jax.numpy as jnp
from jax import lax
from jax.experimental import pallas as pl
from jax.experimental.pallas import tpu as pltpu
from jax.sharding import PartitionSpec as P

MESH = pl.DeviceIdType.MESH
F32 = jnp.float32
BF16 = jnp.bfloat16
VEC = 8
DEG = 4
BS = 128
K = 5
G = 4


def split(value):
    high = value.astype(BF16)
    low = (value - high.astype(F32)).astype(BF16)
    return high, low


def reach_steps(wide):
    steps, reach = [], 1
    while 2 * reach < wide:
        steps.append(reach)
        reach *= 2
    return steps


def kernel(
    wide,
    nodes,
    slab,
    hblocks,
    blist,
    rotation,
    out,
    slab_in,
    h_in,
    codes_in,
    codes_sm,
    position_sm,
    hs,
    fields,
    halo,
    xs,
    fin,
    recv,
    both_last,
    gram_all,
    gram_out,
    gram_in,
    rot_in,
    rot_wide,
    mixer,
    local_sem,
    slab_send,
    slab_recv,
    codes_send,
    codes_recv,
    h_send,
    h_recv,
    halo_send,
    halo_recv,
    fin_send,
    fin_recv,
    gram_send,
    gram_recv,
    reach_sem,
):
    w = lax.axis_index("wide")
    g = lax.axis_index("grp")
    nb = wide // G
    chunk = VEC * nb
    steps = reach_steps(wide)
    source = w // nb
    is_own = source == g
    has_left = w > 0
    has_right = w < wide - 1

    def remote(src, dst, send_sem, recv_sem, to):
        return pltpu.make_async_remote_copy(
            src_ref=src, dst_ref=dst, send_sem=send_sem, recv_sem=recv_sem, device_id=to, device_id_type=MESH
        )

    def arrived(ref, sem):
        pltpu.make_async_copy(ref, ref, sem).wait()

    def row_at(d):
        return lax.rem(g + d, G)

    def at_offset(d):
        return lax.rem(w + d, wide)

    barrier = pltpu.get_barrier_semaphore()
    for d in range(1, G):
        pl.semaphore_signal(barrier, inc=1, device_id=(w, row_at(d)), device_id_type=MESH)

    for to in (at_offset(1), at_offset(wide - 1)):
        pl.semaphore_signal(barrier, inc=1, device_id=(to, g), device_id_type=MESH)

    own_slab = pltpu.make_async_copy(slab.at[pl.ds(g * 2 * chunk, 2 * chunk)], slab_in.at[g], local_sem.at[0])
    own_slab.start()
    own_h = pltpu.make_async_copy(hblocks, h_in.at[g], local_sem.at[1])
    own_h.start()
    own_codes = pltpu.make_async_copy(blist.at[0], codes_in.at[g], local_sem.at[2])
    own_codes.start()
    own_rot = pltpu.make_async_copy(rotation, rot_in, local_sem.at[3])
    own_rot.start()

    zero = jnp.zeros((2 * chunk, BS), BF16)
    for parity in range(2):
        for col in range(4):
            xs[parity, col] = zero
            xs[parity, 20 + col] = zero

        @pl.when(jnp.logical_not(has_left))
        def _():
            for r in range(G):
                xs[parity, (r + 1) * 4] = zero

        @pl.when(jnp.logical_not(has_right))
        def _():
            for r in range(G):
                xs[parity, (r + 1) * 4 + 3] = zero

    pl.semaphore_wait(barrier, G + 1)

    def greet(i):
        for to in (at_offset(steps[i]), at_offset(wide - steps[i])):
            pl.semaphore_signal(reach_sem.at[i], inc=1, device_id=(to, g), device_id_type=MESH)

    def greeted(i):
        pl.semaphore_wait(reach_sem.at[i], 2)
        if i + 1 < len(steps):
            greet(i + 1)

    greet(0)

    def slab_copy(d):
        to = row_at(d)
        return remote(
            slab.at[pl.ds(to * 2 * chunk, 2 * chunk)], slab_in.at[g], slab_send.at[d], slab_recv.at[g], (w, to)
        )

    def codes_copy(d):
        return remote(blist.at[0], codes_in.at[g], codes_send.at[d], codes_recv.at[g], (w, row_at(d)))

    def h_copy(half, d):
        return remote(
            hblocks.at[half], h_in.at[g, half], h_send.at[half, d // 2], h_recv.at[g, half], (w, row_at(d))
        )

    def h_forward(half, d):
        origin = row_at(G - d)
        return remote(
            h_in.at[origin, half], h_in.at[origin, half], h_send.at[half, 2], h_recv.at[origin, half], (w, row_at(d))
        )

    for d in (1, 3, 2):
        slab_copy(d).start()
    for d in (1, 3, 2):
        codes_copy(d).start()
    h_copy(0, 1).start()
    h_copy(1, 3).start()
    h_copy(1, 1).start()
    h_copy(0, 3).start()

    def split_h(r):
        @pl.loop(0, 2)
        def _(q):
            for k in range(K):
                high, low = split(h_in[r, q, k])
                hs[r, q, 0:BS, k * BS : (k + 1) * BS] = high
                hs[r, q, BS : 2 * BS, k * BS : (k + 1) * BS] = low

    def store_split(parity, position, value):
        high, low = split(value)
        xs[parity, position, 0:chunk] = high
        xs[parity, position, chunk : 2 * chunk] = low

    def halo_copy(n, r, side):
        to = w - 1 if side == 0 else w + 1
        return remote(
            fields.at[n, r, side],
            halo.at[n, r, 1 - side],
            halo_send.at[n, r, side],
            halo_recv.at[n, r, 1 - side],
            (to, g),
        )

    def send_halos(n, r):
        @pl.when(has_left)
        def _():
            halo_copy(n, r, 0).start()

        @pl.when(has_right)
        def _():
            halo_copy(n, r, 1).start()

    def take_halos(n):
        parity = n % 2

        @pl.loop(0, G)
        def _(r):
            @pl.when(has_left)
            def _():
                halo_copy(n, r, 1).wait_recv()
                store_split(parity, (r + 1) * 4, halo[n, r, 0])

            @pl.when(has_right)
            def _():
                halo_copy(n, r, 0).wait_recv()
                store_split(parity, (r + 1) * 4 + 3, halo[n, r, 1])

    def product(n, r, q):
        parity = n % 2
        picked = [xs[parity, r * 4 + position_sm[r, q * 8 + k]] for k in range(K)]
        both = jnp.concatenate(picked, axis=1)
        p = lax.dot_general(both, hs[r, q], (((1,), (1,)), ((), ())), preferred_element_type=F32)
        small = p[:chunk, BS:] + p[chunk:, :BS] + p[chunk:, BS:]
        return p[:chunk, :BS] + small

    def apply_row(n, r):
        for q in range(2):
            value = product(n, r, q)
            if n > 0:
                value = 2.0 * value - fields[n - 1, r, q]
            if n + 1 < DEG:
                fields[n + 1, r, q] = value
                store_split((n + 1) % 2, (r + 1) * 4 + 1 + q, value)
            else:
                fin[r, :, q * VEC : (q + 1) * VEC, :] = value.reshape(nb, VEC, BS)
                high, low = split(value)
                both_last[0:chunk, q * BS : (q + 1) * BS] = high
                both_last[chunk : 2 * chunk, q * BS : (q + 1) * BS] = low
        if n + 1 < DEG:
            send_halos(n + 1, r)

    own_h.wait()
    split_h(g)
    own_rot.wait()
    mine = lax.broadcasted_iota(jnp.int32, (VEC, wide), 1) == w
    for c in range(VEC):
        column = jnp.sum(jnp.where(mine, rot_in[c], 0.0), axis=1, keepdims=True)
        for a in range(VEC):
            rot_wide[c * VEC + a] = jnp.broadcast_to(column[a : a + 1, :], (VEC, BS))

    def start_row(r):
        for q in range(2):
            value = slab_in[r, pl.ds(q, chunk, stride=2), :]
            fields[0, r, q] = value
            store_split(0, (r + 1) * 4 + 1 + q, value)
        send_halos(0, r)

    own_slab.wait()
    start_row(g)
    for d in (1, 3, 2):
        arrived(slab_in.at[row_at(d)], slab_recv.at[row_at(d)])
        start_row(row_at(d))

    own_codes.wait()
    for d in (1, 3, 2):
        arrived(codes_in.at[row_at(d)], codes_recv.at[row_at(d)])
    to_scalars = pltpu.make_async_copy(codes_in, codes_sm, local_sem.at[4])
    to_scalars.start()
    to_scalars.wait()
    for r in range(G):
        for q in range(2):
            for k in range(K):
                code = codes_sm[r, q, k]
                line = (code * 11) >> 5
                position_sm[r, q * 8 + k] = line * 4 + code - 3 * line + q

    def h_wait(d, half):
        r = row_at(d)
        arrived(h_in.at[r, half], h_recv.at[r, half])

    waiting = list(range(len(steps)))

    def next_round():
        if waiting:
            greeted(waiting.pop(0))

    next_round()
    take_halos(0)
    apply_row(0, g)
    next_round()
    h_wait(3, 0)
    h_forward(0, 1).start()
    h_wait(1, 1)
    h_forward(1, 3).start()
    next_round()
    h_wait(3, 1)
    split_h(row_at(3))
    apply_row(0, row_at(3))
    next_round()
    h_wait(1, 0)
    split_h(row_at(1))
    apply_row(0, row_at(1))
    while waiting:
        next_round()
    h_wait(2, 0)
    h_wait(2, 1)
    split_h(row_at(2))
    apply_row(0, row_at(2))

    for n in range(1, DEG - 1):
        take_halos(n)

        @pl.loop(0, G)
        def _(r):
            apply_row(n, r)

    take_halos(DEG - 1)

    def to_owners(r, block_copy, local_copy):
        @pl.loop(0, nb)
        def _(i):
            b = lax.rem(i + w, nb)
            to = g * nb + b
            own = jnp.logical_and(to == w, r == g)

            @pl.when(jnp.logical_not(own))
            def _():
                block_copy(b, (to, r)).start()

            @pl.when(own)
            def _():
                local_copy(b).start()

    gram_all[...] = jnp.zeros_like(gram_all)

    @pl.loop(0, G)
    def _(d):
        r = row_at(d)
        apply_row(DEG - 1, r)
        slot = recv.at[pl.ds(w * 2 * VEC, 2 * VEC)]
        to_owners(
            r,
            lambda b, to: remote(fin.at[r, b], slot, fin_send.at[0], fin_recv.at[0], to),
            lambda b: pltpu.make_async_copy(fin.at[r, b], slot, fin_recv.at[0]),
        )
        both = both_last[...]
        gram_all[...] += lax.dot_general(both, both, (((1,), (1,)), ((), ())), preferred_element_type=F32)

    states_gram = (gram_all[:chunk, chunk:] + gram_all[chunk:, :chunk] + gram_all[chunk:, chunk:]) + gram_all[:chunk, :chunk]
    row_id = lax.broadcasted_iota(jnp.int32, (chunk, chunk), 0)
    lane_id = lax.broadcasted_iota(jnp.int32, (chunk, chunk), 1)
    states_gram = jnp.where(row_id // VEC == lane_id // VEC, states_gram, 0.0)
    fold_row = lax.broadcasted_iota(jnp.int32, (chunk, BS), 0)
    fold_lane = lax.broadcasted_iota(jnp.int32, (chunk, BS), 1)
    fold = jnp.where(fold_row % VEC == fold_lane % VEC, 1.0, 0.0).astype(F32)
    folded = jnp.dot(states_gram, fold, precision=lax.Precision.HIGHEST, preferred_element_type=F32)
    folded = jnp.where(fold_row % VEC == fold_lane // VEC, folded, 0.0)
    flat = jnp.sum(folded.reshape(nb, VEC, BS), axis=1)
    for b in range(nb):
        gram_out[b] = flat[b : b + 1, :]

    @pl.loop(0, G)
    def _(d):
        r = row_at(d)
        to_owners(
            r,
            lambda b, to: remote(gram_out.at[b], gram_in.at[w], gram_send.at[0], gram_recv.at[0], to),
            lambda b: pltpu.make_async_copy(gram_out.at[b], gram_in.at[w], gram_recv.at[0]),
        )

    arrived(gram_in, gram_recv.at[0])
    whole = jnp.sum(gram_in[...], axis=0) * (1.0 / nodes)

    entry = {}
    for a in range(VEC):
        for c in range(a + 1):
            i = a * VEC + c
            entry[a, c] = jnp.broadcast_to(whole[:, i : i + 1], (VEC, BS))
    groups = 2 * wide // VEC

    def tiles(group):
        return [recv[pl.ds(group * VEC * VEC + s, VEC, stride=VEC), :] for s in range(VEC)]

    lower, inverse = {}, []
    for j in range(VEC):
        rest = entry[j, j]
        for k in range(j):
            rest = rest - lower[j, k] * lower[j, k]
        root = lax.rsqrt(rest)
        root = root * (1.5 - 0.5 * rest * root * root)
        inverse.append(root)
        for i in range(j + 1, VEC):
            value = entry[i, j]
            for k in range(j):
                value = value - lower[i, k] * lower[j, k]
            lower[i, j] = value * root
    for a in range(VEC):
        row = {}
        for c in reversed(range(VEC)):
            value = rot_wide[c * VEC + a]
            for k in range(c + 1, VEC):
                value = value - row[k] * lower[k, c]
            row[c] = value * inverse[c]
            mixer[a * VEC + c] = row[c]

    arrived(recv, fin_recv.at[0])

    @pl.loop(0, groups)
    def _(group):
        x = tiles(group)
        for a in range(VEC):
            value = mixer[a * VEC] * x[0]
            for c in range(1, VEC):
                value = value + mixer[a * VEC + c] * x[c]
            out[a, 0, pl.ds(pl.multiple_of(group * VEC, VEC), VEC), :] = value

    for d in range(1, G):
        slab_copy(d).wait_send()
        codes_copy(d).wait_send()
    for half in range(2):
        h_copy(half, 1).wait_send()
        h_copy(half, 3).wait_send()
    h_forward(0, 1).wait_send()
    h_forward(1, 3).wait_send()

    @pl.loop(0, DEG)
    def _(n):
        @pl.loop(0, G)
        def _(r):
            @pl.when(has_left)
            def _():
                halo_copy(n, r, 0).wait_send()

            @pl.when(has_right)
            def _():
                halo_copy(n, r, 1).wait_send()

    @pl.when(is_own)
    def _():
        part = recv.at[pl.ds(0, (wide - 1) * 2 * VEC)]
        arrived(part, fin_send.at[0])
        part = gram_in.at[pl.ds(0, wide - 1)]
        arrived(part, gram_send.at[0])

    @pl.when(jnp.logical_not(is_own))
    def _():
        arrived(recv, fin_send.at[0])
        arrived(gram_in, gram_send.at[0])


def body(slab, hblocks, blist, rotation):
    wide = lax.axis_size("wide")
    states = slab.shape[0]
    chunk = states // G
    nb = wide // G
    nodes = G * 2 * wide * BS
    dma = pltpu.SemaphoreType.DMA
    any_space = pl.BlockSpec(memory_space=pl.ANY)
    return pl.pallas_call(
        functools.partial(kernel, wide, nodes),
        out_shape=jax.ShapeDtypeStruct((VEC, 1, 2 * wide, BS), F32),
        in_specs=[any_space, any_space, any_space, any_space],
        out_specs=pl.BlockSpec(memory_space=pltpu.VMEM),
        scratch_shapes=[
            pltpu.VMEM((G, 2 * chunk, BS), F32),
            pltpu.VMEM((G, 2, K, BS, BS), F32),
            pltpu.VMEM((G, 2, K), jnp.int32),
            pltpu.SMEM((G, 2, K), jnp.int32),
            pltpu.SMEM((G, 16), jnp.int32),
            pltpu.VMEM((G, 2, 2 * BS, K * BS), BF16),
            pltpu.VMEM((DEG, G, 2, chunk, BS), F32),
            pltpu.VMEM((DEG, G, 2, chunk, BS), F32),
            pltpu.VMEM((2, 24, 2 * chunk, BS), BF16),
            pltpu.VMEM((G, nb, 2 * VEC, BS), F32),
            pltpu.VMEM((wide * 2 * VEC, BS), F32),
            pltpu.VMEM((2 * chunk, 2 * BS), BF16),
            pltpu.VMEM((2 * chunk, 2 * chunk), F32),
            pltpu.VMEM((nb, 1, BS), F32),
            pltpu.VMEM((wide, 1, BS), F32),
            pltpu.VMEM((VEC, VEC, wide), F32),
            pltpu.VMEM((VEC * VEC, VEC, BS), F32),
            pltpu.VMEM((VEC * VEC, VEC, BS), F32),
            dma((5,)),
            dma((G,)),
            dma((G,)),
            dma((G,)),
            dma((G,)),
            dma((2, 3)),
            dma((G, 2)),
            dma((DEG, G, 2)),
            dma((DEG, G, 2)),
            dma((1,)),
            dma((1,)),
            dma((1,)),
            dma((1,)),
            pltpu.SemaphoreType.REGULAR((max(1, len(reach_steps(wide))),)),
        ],
        compiler_params=pltpu.CompilerParams(
            collective_id=0, has_side_effects=True, vmem_limit_bytes=60 * 1024 * 1024
        ),
        cost_estimate=pl.CostEstimate(flops=3 * 10**9, bytes_accessed=2 * 1024 * 1024, transcendentals=0),
    )(slab.reshape(2 * states, BS), hblocks.reshape(2, K, BS, BS), blist, jnp.transpose(rotation, (1, 2, 0)))


def solution(mesh):
    in_specs = (
        P(None, "grp", "wide", None),
        P("grp", "wide", None, None, None),
        P("grp", "wide", None),
        P(),
    )
    out_specs = P("wide", "grp", None, None)
    return jax.shard_map(body, mesh=mesh, in_specs=in_specs, out_specs=out_specs, check_vma=False)
```

```python
import functools

import jax
import jax.numpy as jnp
from jax import lax
from jax.experimental import pallas as pl
from jax.experimental.pallas import tpu as pltpu
from jax.sharding import PartitionSpec as P

MESH = pl.DeviceIdType.MESH
F32 = jnp.float32
BF16 = jnp.bfloat16
VEC = 8
DEG = 4
BS = 128
K = 5
G = 4


def split(value):
    high = value.astype(BF16)
    low = (value - high.astype(F32)).astype(BF16)
    return high, low


def reach_steps(wide):
    steps, reach = [], 1
    while 2 * reach < wide:
        steps.append(reach)
        reach *= 2
    return steps


def kernel(
    wide,
    nodes,
    slab,
    hblocks,
    blist,
    rotation,
    out,
    slab_in,
    h_in,
    codes_in,
    codes_sm,
    position_sm,
    hs,
    fields,
    halo,
    xs,
    fin,
    recv,
    both_last,
    gram_all,
    gram_out,
    gram_in,
    rot_in,
    rot_wide,
    mixer,
    local_sem,
    slab_send,
    slab_recv,
    codes_send,
    codes_recv,
    h_send,
    h_recv,
    halo_send,
    halo_recv,
    fin_send,
    fin_recv,
    gram_send,
    gram_recv,
    reach_sem,
):
    w = lax.axis_index("wide")
    g = lax.axis_index("grp")
    nb = wide // G
    chunk = VEC * nb
    steps = reach_steps(wide)
    source = w // nb
    is_own = source == g
    has_left = w > 0
    has_right = w < wide - 1

    def remote(src, dst, send_sem, recv_sem, to):
        return pltpu.make_async_remote_copy(
            src_ref=src, dst_ref=dst, send_sem=send_sem, recv_sem=recv_sem, device_id=to, device_id_type=MESH
        )

    def arrived(ref, sem):
        pltpu.make_async_copy(ref, ref, sem).wait()

    def row_at(d):
        return lax.rem(g + d, G)

    def at_offset(d):
        return lax.rem(w + d, wide)

    barrier = pltpu.get_barrier_semaphore()
    for d in range(1, G):
        pl.semaphore_signal(barrier, inc=1, device_id=(w, row_at(d)), device_id_type=MESH)

    for to in (at_offset(1), at_offset(wide - 1)):
        pl.semaphore_signal(barrier, inc=1, device_id=(to, g), device_id_type=MESH)

    own_slab = pltpu.make_async_copy(slab.at[pl.ds(g * 2 * chunk, 2 * chunk)], slab_in.at[g], local_sem.at[0])
    own_slab.start()
    own_h = pltpu.make_async_copy(hblocks, h_in.at[g], local_sem.at[1])
    own_h.start()
    own_codes = pltpu.make_async_copy(blist.at[0], codes_in.at[g], local_sem.at[2])
    own_codes.start()
    own_rot = pltpu.make_async_copy(rotation, rot_in, local_sem.at[3])
    own_rot.start()

    zero = jnp.zeros((2 * chunk, BS), BF16)
    for n in range(DEG):
        for col in range(4):
            xs[n, col] = zero
            xs[n, 20 + col] = zero

        @pl.when(jnp.logical_not(has_left))
        def _():
            for r in range(G):
                xs[n, (r + 1) * 4] = zero

        @pl.when(jnp.logical_not(has_right))
        def _():
            for r in range(G):
                xs[n, (r + 1) * 4 + 3] = zero

    pl.semaphore_wait(barrier, G + 1)

    def greet(i):
        for to in (at_offset(steps[i]), at_offset(wide - steps[i])):
            pl.semaphore_signal(reach_sem.at[i], inc=1, device_id=(to, g), device_id_type=MESH)

    def greeted(i):
        pl.semaphore_wait(reach_sem.at[i], 2)
        if i + 1 < len(steps):
            greet(i + 1)

    greet(0)

    def slab_copy(d):
        to = row_at(d)
        return remote(
            slab.at[pl.ds(to * 2 * chunk, 2 * chunk)], slab_in.at[g], slab_send.at[d], slab_recv.at[g], (w, to)
        )

    def codes_copy(d):
        return remote(blist.at[0], codes_in.at[g], codes_send.at[d], codes_recv.at[g], (w, row_at(d)))

    def h_copy(half, d):
        return remote(
            hblocks.at[half], h_in.at[g, half], h_send.at[half, d // 2], h_recv.at[g, half], (w, row_at(d))
        )

    def h_forward(half, d):
        origin = row_at(G - d)
        return remote(
            h_in.at[origin, half], h_in.at[origin, half], h_send.at[half, 2], h_recv.at[origin, half], (w, row_at(d))
        )

    for d in (1, 3, 2):
        slab_copy(d).start()
    for d in (1, 3, 2):
        codes_copy(d).start()
    h_copy(0, 1).start()
    h_copy(1, 3).start()
    h_copy(1, 1).start()
    h_copy(0, 3).start()

    def split_h(r):
        @pl.loop(0, 2)
        def _(q):
            for k in range(K):
                high, low = split(h_in[r, q, k])
                hs[r, q, 0:BS, k * BS : (k + 1) * BS] = high
                hs[r, q, BS : 2 * BS, k * BS : (k + 1) * BS] = low

    def store_split(n, position, value):
        high, low = split(value)
        xs[n, position, 0:chunk] = high
        xs[n, position, chunk : 2 * chunk] = low

    def halo_copy(n, r, side):
        to = w - 1 if side == 0 else w + 1
        return remote(
            fields.at[n, r, side],
            halo.at[n, r, 1 - side],
            halo_send.at[n, r, side],
            halo_recv.at[n, r, 1 - side],
            (to, g),
        )

    def send_halos(n, r):
        @pl.when(has_left)
        def _():
            halo_copy(n, r, 0).start()

        @pl.when(has_right)
        def _():
            halo_copy(n, r, 1).start()

    def take_halos(n, r):
        @pl.when(has_left)
        def _():
            halo_copy(n, r, 1).wait_recv()
            store_split(n, (r + 1) * 4, halo[n, r, 0])

        @pl.when(has_right)
        def _():
            halo_copy(n, r, 0).wait_recv()
            store_split(n, (r + 1) * 4 + 3, halo[n, r, 1])

    def product(n, r, q):
        picked = [xs[n, r * 4 + position_sm[r, q * 8 + k]] for k in range(K)]
        both = jnp.concatenate(picked, axis=1)
        p = lax.dot_general(both, hs[r, q], (((1,), (1,)), ((), ())), preferred_element_type=F32)
        small = p[:chunk, BS:] + p[chunk:, :BS] + p[chunk:, BS:]
        return p[:chunk, :BS] + small

    def apply_row(n, r):
        for q in range(2):
            value = product(n, r, q)
            if n > 0:
                value = 2.0 * value - fields[n - 1, r, q]
            if n + 1 < DEG:
                fields[n + 1, r, q] = value
                store_split(n + 1, (r + 1) * 4 + 1 + q, value)
            else:
                fin[r, :, q * VEC : (q + 1) * VEC, :] = value.reshape(nb, VEC, BS)
                high, low = split(value)
                both_last[0:chunk, q * BS : (q + 1) * BS] = high
                both_last[chunk : 2 * chunk, q * BS : (q + 1) * BS] = low
        if n + 1 < DEG:
            send_halos(n + 1, r)

    own_h.wait()
    split_h(g)
    own_rot.wait()
    mine = lax.broadcasted_iota(jnp.int32, (VEC, wide), 1) == w
    for c in range(VEC):
        column = jnp.sum(jnp.where(mine, rot_in[c], 0.0), axis=1, keepdims=True)
        for a in range(VEC):
            rot_wide[c * VEC + a] = jnp.broadcast_to(column[a : a + 1, :], (VEC, BS))

    def start_row(r):
        for q in range(2):
            value = slab_in[r, pl.ds(q, chunk, stride=2), :]
            fields[0, r, q] = value
            store_split(0, (r + 1) * 4 + 1 + q, value)
        send_halos(0, r)

    own_slab.wait()
    start_row(g)
    for d in (1, 3, 2):
        arrived(slab_in.at[row_at(d)], slab_recv.at[row_at(d)])
        start_row(row_at(d))

    own_codes.wait()
    for d in (1, 3, 2):
        arrived(codes_in.at[row_at(d)], codes_recv.at[row_at(d)])
    to_scalars = pltpu.make_async_copy(codes_in, codes_sm, local_sem.at[4])
    to_scalars.start()
    to_scalars.wait()
    for r in range(G):
        for q in range(2):
            for k in range(K):
                code = codes_sm[r, q, k]
                line = (code * 11) >> 5
                position_sm[r, q * 8 + k] = line * 4 + code - 3 * line + q

    def h_wait(d, half):
        r = row_at(d)
        arrived(h_in.at[r, half], h_recv.at[r, half])

    waiting = list(range(len(steps)))

    def next_round():
        if waiting:
            greeted(waiting.pop(0))

    next_round()

    @pl.loop(0, G)
    def _(r):
        take_halos(0, r)

    apply_row(0, g)
    next_round()
    h_wait(3, 0)
    h_forward(0, 1).start()
    h_wait(1, 1)
    h_forward(1, 3).start()
    next_round()
    h_wait(3, 1)
    split_h(row_at(3))
    apply_row(0, row_at(3))
    next_round()
    h_wait(1, 0)
    split_h(row_at(1))
    apply_row(0, row_at(1))
    while waiting:
        next_round()
    for d in (0, 3, 1):
        take_halos(1, row_at(d))
    apply_row(1, g)
    h_wait(2, 0)
    h_wait(2, 1)
    split_h(row_at(2))
    apply_row(0, row_at(2))

    take_halos(1, row_at(2))

    @pl.loop(0, G)
    def _(r):
        @pl.when(r != g)
        def _():
            apply_row(1, r)

    def wave(n, then):
        take_halos(n, 0)

        @pl.loop(0, G)
        def _(r):
            @pl.when(r < G - 1)
            def _():
                take_halos(n, r + 1)

            apply_row(n, r)
            then(r)

    for n in range(2, DEG - 1):
        wave(n, lambda r: None)

    cores = min(2, nb)
    ring = nb // cores
    offsets = sorted(range(ring), key=lambda d: -min(d, ring - d))
    far = [d for d in offsets if min(d, ring - d) > 1]
    near = [d for d in offsets if min(d, ring - d) <= 1]

    def to_owners(r, distances, block_copy, local_copy):
        place = lax.rem(w, nb)
        for d in distances:
            for other in reversed(range(cores)):
                b = lax.rem(place // cores + d, ring) * cores + lax.rem(place + other, cores)
                to = g * nb + b
                if d == 0 and other == 0:
                    own = jnp.logical_and(to == w, r == g)

                    @pl.when(jnp.logical_not(own))
                    def _():
                        block_copy(b, (to, r)).start()

                    @pl.when(own)
                    def _():
                        local_copy(b).start()

                else:
                    block_copy(b, (to, r)).start()

    def send_blocks(r, distances):
        slot = recv.at[pl.ds(w * 2 * VEC, 2 * VEC)]
        to_owners(
            r,
            distances,
            lambda b, to: remote(fin.at[r, b], slot, fin_send.at[0], fin_recv.at[0], to),
            lambda b: pltpu.make_async_copy(fin.at[r, b], slot, fin_recv.at[0]),
        )

    gram_all[...] = jnp.zeros_like(gram_all)

    def last(r):
        send_blocks(r, far)
        both = both_last[...]
        gram_all[...] += lax.dot_general(both, both, (((1,), (1,)), ((), ())), preferred_element_type=F32)

    wave(DEG - 1, last)

    states_gram = (gram_all[:chunk, chunk:] + gram_all[chunk:, :chunk] + gram_all[chunk:, chunk:]) + gram_all[:chunk, :chunk]
    row_id = lax.broadcasted_iota(jnp.int32, (chunk, chunk), 0)
    lane_id = lax.broadcasted_iota(jnp.int32, (chunk, chunk), 1)
    states_gram = jnp.where(row_id // VEC == lane_id // VEC, states_gram, 0.0)
    fold_row = lax.broadcasted_iota(jnp.int32, (chunk, BS), 0)
    fold_lane = lax.broadcasted_iota(jnp.int32, (chunk, BS), 1)
    fold = jnp.where(fold_row % VEC == fold_lane % VEC, 1.0, 0.0).astype(F32)
    folded = jnp.dot(states_gram, fold, precision=lax.Precision.HIGHEST, preferred_element_type=F32)
    folded = jnp.where(fold_row % VEC == fold_lane // VEC, folded, 0.0)
    flat = jnp.sum(folded.reshape(nb, VEC, BS), axis=1)
    for b in range(nb):
        gram_out[b] = flat[b : b + 1, :]

    @pl.loop(0, G)
    def _(d):
        r = row_at(d)
        to_owners(
            r,
            offsets,
            lambda b, to: remote(gram_out.at[b], gram_in.at[w], gram_send.at[0], gram_recv.at[0], to),
            lambda b: pltpu.make_async_copy(gram_out.at[b], gram_in.at[w], gram_recv.at[0]),
        )

    @pl.loop(0, G)
    def _(r):
        send_blocks(r, near)

    arrived(gram_in, gram_recv.at[0])
    whole = jnp.sum(gram_in[...], axis=0) * (1.0 / nodes)

    entry = {}
    for a in range(VEC):
        for c in range(a + 1):
            i = a * VEC + c
            entry[a, c] = jnp.broadcast_to(whole[:, i : i + 1], (VEC, BS))
    groups = 2 * wide // VEC

    def tiles(group):
        return [recv[pl.ds(group * VEC * VEC + s, VEC, stride=VEC), :] for s in range(VEC)]

    lower, inverse = {}, []
    for j in range(VEC):
        rest = entry[j, j]
        for k in range(j):
            rest = rest - lower[j, k] * lower[j, k]
        root = lax.rsqrt(rest)
        root = root * (1.5 - 0.5 * rest * root * root)
        inverse.append(root)
        for i in range(j + 1, VEC):
            value = entry[i, j]
            for k in range(j):
                value = value - lower[i, k] * lower[j, k]
            lower[i, j] = value * root
    for a in range(VEC):
        row = {}
        for c in reversed(range(VEC)):
            value = rot_wide[c * VEC + a]
            for k in range(c + 1, VEC):
                value = value - row[k] * lower[k, c]
            row[c] = value * inverse[c]
            mixer[a * VEC + c] = row[c]

    arrived(recv, fin_recv.at[0])

    @pl.loop(0, groups)
    def _(group):
        x = tiles(group)
        for a in range(VEC):
            value = mixer[a * VEC] * x[0]
            for c in range(1, VEC):
                value = value + mixer[a * VEC + c] * x[c]
            out[a, 0, pl.ds(pl.multiple_of(group * VEC, VEC), VEC), :] = value

    for d in range(1, G):
        slab_copy(d).wait_send()
        codes_copy(d).wait_send()
    for half in range(2):
        h_copy(half, 1).wait_send()
        h_copy(half, 3).wait_send()
    h_forward(0, 1).wait_send()
    h_forward(1, 3).wait_send()

    @pl.loop(0, DEG)
    def _(n):
        @pl.loop(0, G)
        def _(r):
            @pl.when(has_left)
            def _():
                halo_copy(n, r, 0).wait_send()

            @pl.when(has_right)
            def _():
                halo_copy(n, r, 1).wait_send()

    @pl.when(is_own)
    def _():
        part = recv.at[pl.ds(0, (wide - 1) * 2 * VEC)]
        arrived(part, fin_send.at[0])
        part = gram_in.at[pl.ds(0, wide - 1)]
        arrived(part, gram_send.at[0])

    @pl.when(jnp.logical_not(is_own))
    def _():
        arrived(recv, fin_send.at[0])
        arrived(gram_in, gram_send.at[0])


def body(slab, hblocks, blist, rotation):
    wide = lax.axis_size("wide")
    states = slab.shape[0]
    chunk = states // G
    nb = wide // G
    nodes = G * 2 * wide * BS
    dma = pltpu.SemaphoreType.DMA
    any_space = pl.BlockSpec(memory_space=pltpu.HBM)
    operands = (slab.reshape(2 * states, BS), hblocks.reshape(2, K, BS, BS), blist, jnp.transpose(rotation, (1, 2, 0)))
    operands = [pltpu.with_memory_space_constraint(value, pltpu.HBM) for value in operands]
    return pl.pallas_call(
        functools.partial(kernel, wide, nodes),
        out_shape=jax.ShapeDtypeStruct((VEC, 1, 2 * wide, BS), F32),
        in_specs=[any_space, any_space, any_space, any_space],
        out_specs=pl.BlockSpec(memory_space=pltpu.VMEM),
        scratch_shapes=[
            pltpu.VMEM((G, 2 * chunk, BS), F32),
            pltpu.VMEM((G, 2, K, BS, BS), F32),
            pltpu.VMEM((G, 2, K), jnp.int32),
            pltpu.SMEM((G, 2, K), jnp.int32),
            pltpu.SMEM((G, 16), jnp.int32),
            pltpu.VMEM((G, 2, 2 * BS, K * BS), BF16),
            pltpu.VMEM((DEG, G, 2, chunk, BS), F32),
            pltpu.VMEM((DEG, G, 2, chunk, BS), F32),
            pltpu.VMEM((DEG, 24, 2 * chunk, BS), BF16),
            pltpu.VMEM((G, nb, 2 * VEC, BS), F32),
            pltpu.VMEM((wide * 2 * VEC, BS), F32),
            pltpu.VMEM((2 * chunk, 2 * BS), BF16),
            pltpu.VMEM((2 * chunk, 2 * chunk), F32),
            pltpu.VMEM((nb, 1, BS), F32),
            pltpu.VMEM((wide, 1, BS), F32),
            pltpu.VMEM((VEC, VEC, wide), F32),
            pltpu.VMEM((VEC * VEC, VEC, BS), F32),
            pltpu.VMEM((VEC * VEC, VEC, BS), F32),
            dma((5,)),
            dma((G,)),
            dma((G,)),
            dma((G,)),
            dma((G,)),
            dma((2, 3)),
            dma((G, 2)),
            dma((DEG, G, 2)),
            dma((DEG, G, 2)),
            dma((1,)),
            dma((1,)),
            dma((1,)),
            dma((1,)),
            pltpu.SemaphoreType.REGULAR((max(1, len(reach_steps(wide))),)),
        ],
        compiler_params=pltpu.CompilerParams(
            collective_id=0, has_side_effects=True, vmem_limit_bytes=40 * 1024 * 1024
        ),
        cost_estimate=pl.CostEstimate(flops=3 * 10**9, bytes_accessed=2 * 1024 * 1024, transcendentals=0),
    )(*operands)


def solution(mesh):
    in_specs = (
        P(None, "grp", "wide", None),
        P("grp", "wide", None, None, None),
        P("grp", "wide", None),
        P(),
    )
    out_specs = P("wide", "grp", None, None)
    return jax.shard_map(body, mesh=mesh, in_specs=in_specs, out_specs=out_specs, check_vma=False)
```

```python
import functools

import jax
import jax.numpy as jnp
from jax import lax
from jax.experimental import pallas as pl
from jax.experimental.pallas import tpu as pltpu
from jax.sharding import PartitionSpec as P

MESH = pl.DeviceIdType.MESH
F32 = jnp.float32
BF16 = jnp.bfloat16
VEC = 8
DEG = 4
BS = 128
K = 5
G = 4


def split(value):
    high = value.astype(BF16)
    low = (value - high.astype(F32)).astype(BF16)
    return high, low


def reach_steps(wide):
    steps, reach = [], 1
    while 2 * reach < wide:
        steps.append(reach)
        reach *= 2
    return steps


def kernel(
    wide,
    nodes,
    slab,
    hblocks,
    blist,
    rotation,
    out,
    slab_in,
    h_in,
    codes_in,
    codes_sm,
    position_sm,
    hs,
    fields,
    halo,
    xs,
    fin,
    recv,
    both_last,
    gram_all,
    gram_out,
    gram_in,
    rot_in,
    rot_wide,
    mixer,
    local_sem,
    slab_send,
    slab_recv,
    codes_send,
    codes_recv,
    h_send,
    h_recv,
    halo_send,
    halo_recv,
    fin_send,
    fin_recv,
    gram_send,
    gram_recv,
    reach_sem,
):
    w = lax.axis_index("wide")
    g = lax.axis_index("grp")
    nb = wide // G
    chunk = VEC * nb
    steps = reach_steps(wide)
    source = w // nb
    is_own = source == g
    has_left = w > 0
    has_right = w < wide - 1
    first = lax.rem(w, 2)
    other = 1 - first

    def remote(src, dst, send_sem, recv_sem, to):
        return pltpu.make_async_remote_copy(
            src_ref=src, dst_ref=dst, send_sem=send_sem, recv_sem=recv_sem, device_id=to, device_id_type=MESH
        )

    def arrived(ref, sem):
        pltpu.make_async_copy(ref, ref, sem).wait()

    def row_at(d):
        return lax.rem(g + d, G)

    def at_offset(d):
        return lax.rem(w + d, wide)

    barrier = pltpu.get_barrier_semaphore()
    for d in range(1, G):
        pl.semaphore_signal(barrier, inc=1, device_id=(w, row_at(d)), device_id_type=MESH)

    for to in (at_offset(1), at_offset(wide - 1)):
        pl.semaphore_signal(barrier, inc=1, device_id=(to, g), device_id_type=MESH)

    own_slab = pltpu.make_async_copy(slab.at[pl.ds(g * 2 * chunk, 2 * chunk)], slab_in.at[g], local_sem.at[0])
    own_slab.start()
    own_h = pltpu.make_async_copy(hblocks, h_in.at[g], local_sem.at[1])
    own_h.start()
    own_codes = pltpu.make_async_copy(blist.at[0], codes_in.at[g], local_sem.at[2])
    own_codes.start()
    own_rot = pltpu.make_async_copy(rotation, rot_in, local_sem.at[3])
    own_rot.start()

    zero = jnp.zeros((2 * chunk, BS), BF16)
    for n in range(DEG):
        for col in range(4):
            xs[n, col] = zero
            xs[n, 20 + col] = zero

        @pl.when(jnp.logical_not(has_left))
        def _():
            for r in range(G):
                xs[n, (r + 1) * 4] = zero

        @pl.when(jnp.logical_not(has_right))
        def _():
            for r in range(G):
                xs[n, (r + 1) * 4 + 3] = zero

    pl.semaphore_wait(barrier, G + 1)

    def greet(i):
        for to in (at_offset(steps[i]), at_offset(wide - steps[i])):
            pl.semaphore_signal(reach_sem.at[i], inc=1, device_id=(to, g), device_id_type=MESH)

    def greeted(i):
        pl.semaphore_wait(reach_sem.at[i], 2)
        if i + 1 < len(steps):
            greet(i + 1)

    greet(0)

    def slab_copy(d):
        to = row_at(d)
        return remote(
            slab.at[pl.ds(to * 2 * chunk, 2 * chunk)], slab_in.at[g], slab_send.at[d], slab_recv.at[g], (w, to)
        )

    def codes_copy(d):
        return remote(blist.at[0], codes_in.at[g], codes_send.at[d], codes_recv.at[g], (w, row_at(d)))

    def h_copy(half, d):
        return remote(
            hblocks.at[half], h_in.at[g, half], h_send.at[half, d // 2], h_recv.at[g, half], (w, row_at(d))
        )

    def h_forward(half):
        d = 1 + 2 * half
        origin = row_at(G - d)
        block = h_in.at[origin, half]
        return remote(block, block, h_send.at[half, 2], h_recv.at[origin, half], (w, row_at(d)))

    for d in (1, 3, 2):
        slab_copy(d).start()
    for d in (1, 3, 2):
        codes_copy(d).start()
    h_copy(0, 1).start()
    h_copy(1, 3).start()
    h_copy(1, 1).start()
    h_copy(0, 3).start()

    def split_column(r, q):
        for k in range(K):
            high, low = split(h_in[r, q, k])
            hs[r, q, 0:BS, k * BS : (k + 1) * BS] = high
            hs[r, q, BS : 2 * BS, k * BS : (k + 1) * BS] = low

    def split_h(r):
        for q in range(2):
            split_column(r, q)

    def store_split(n, position, value):
        high, low = split(value)
        xs[n, position, 0:chunk] = high
        xs[n, position, chunk : 2 * chunk] = low

    def halo_copy(n, r, side):
        return remote(
            fields.at[n, r, side],
            halo.at[n, r, 1 - side],
            halo_send.at[n, r, side],
            halo_recv.at[n, r, 1 - side],
            (w - 1 + 2 * side, g),
        )

    def send_halo(n, r, side):
        to = w - 1 + 2 * side

        @pl.when(jnp.logical_and(to >= 0, to < wide))
        def _():
            halo_copy(n, r, side).start()

    def take_halos(n, r):
        @pl.when(has_left)
        def _():
            halo_copy(n, r, 1).wait_recv()
            store_split(n, (r + 1) * 4, halo[n, r, 0])

        @pl.when(has_right)
        def _():
            halo_copy(n, r, 0).wait_recv()
            store_split(n, (r + 1) * 4 + 3, halo[n, r, 1])

    def product(n, r, q):
        picked = [xs[n, r * 4 + position_sm[r, q * 8 + k]] for k in range(K)]
        both = jnp.concatenate(picked, axis=1)
        p = lax.dot_general(both, hs[r, q], (((1,), (1,)), ((), ())), preferred_element_type=F32)
        small = p[:chunk, BS:] + p[chunk:, :BS] + p[chunk:, BS:]
        return p[:chunk, :BS] + small

    def apply(n, blocks):
        values = []
        for r, q in blocks:
            value = product(n, r, q)
            values.append(2.0 * value - fields[n - 1, r, q] if n > 0 else value)
        for (r, q), value in zip(blocks, values):
            if n + 1 < DEG:
                fields[n + 1, r, q] = value
                store_split(n + 1, (r + 1) * 4 + 1 + q, value)
            else:
                fin[r, :, q * VEC : (q + 1) * VEC, :] = value.reshape(nb, VEC, BS)
                high, low = split(value)
                both_last[r, 0:chunk, q * BS : (q + 1) * BS] = high
                both_last[r, chunk : 2 * chunk, q * BS : (q + 1) * BS] = low
        if n + 1 < DEG:
            for r, q in blocks:
                send_halo(n + 1, r, q)

    own_h.wait()
    split_h(g)
    own_rot.wait()
    mine = lax.broadcasted_iota(jnp.int32, (VEC, wide), 1) == w
    for c in range(VEC):
        column = jnp.sum(jnp.where(mine, rot_in[c], 0.0), axis=1, keepdims=True)
        for a in range(VEC):
            rot_wide[c * VEC + a] = jnp.broadcast_to(column[a : a + 1, :], (VEC, BS))

    def start_row(r):
        for q in range(2):
            value = slab_in[r, pl.ds(q, chunk, stride=2), :]
            fields[0, r, q] = value
            store_split(0, (r + 1) * 4 + 1 + q, value)
        send_halo(0, r, first)
        send_halo(0, r, other)

    own_slab.wait()
    start_row(g)
    for d in (1, 3, 2):
        arrived(slab_in.at[row_at(d)], slab_recv.at[row_at(d)])
        start_row(row_at(d))

    own_codes.wait()
    for d in (1, 3, 2):
        arrived(codes_in.at[row_at(d)], codes_recv.at[row_at(d)])
    to_scalars = pltpu.make_async_copy(codes_in, codes_sm, local_sem.at[4])
    to_scalars.start()
    to_scalars.wait()
    for r in range(G):
        for q in range(2):
            for k in range(K):
                code = codes_sm[r, q, k]
                line = (code * 11) >> 5
                position_sm[r, q * 8 + k] = line * 4 + code - 3 * line + q

    def h_wait(d, half):
        r = row_at(d)
        arrived(h_in.at[r, half], h_recv.at[r, half])

    waiting = list(range(len(steps)))

    def next_round():
        if waiting:
            greeted(waiting.pop(0))

    next_round()

    @pl.loop(0, G)
    def _(r):
        take_halos(0, r)

    apply(0, [(g, first), (g, other)])
    next_round()

    h_wait(G - 1 - 2 * first, first)
    h_forward(first).start()
    h_wait(G - 1 - 2 * other, other)
    next_round()
    h_wait(3, 1)
    h_forward(other).start()
    split_h(row_at(3))
    apply(0, [(row_at(3), first), (row_at(3), other)])
    next_round()
    h_wait(1, 0)
    split_h(row_at(1))
    apply(0, [(row_at(1), first), (row_at(1), other)])
    while waiting:
        next_round()
    for d in (0, 3, 1):
        take_halos(1, row_at(d))
    apply(1, [(g, first), (g, other)])
    for q in (first, other):
        h_wait(2, q)
        split_column(row_at(2), q)
        apply(0, [(row_at(2), q)])

    take_halos(1, row_at(2))
    for q in (first, other):
        apply(1, [(row_at(d), q) for d in (3, 1, 2)])

    for r in range(3):
        take_halos(2, r)
    apply(2, [(0, first), (1, first)])
    take_halos(2, 3)
    apply(2, [(2, first), (3, first)])
    apply(2, [(r, other) for r in range(G)])

    cores = min(2, nb)
    ring = nb // cores
    offsets = sorted(range(ring), key=lambda d: -min(d, ring - d))
    far = [d for d in offsets if min(d, ring - d) > 1]
    near = [d for d in offsets if min(d, ring - d) <= 1]

    def to_owners(r, distances, block_copy, local_copy):
        place = lax.rem(w, nb)
        for d in distances:
            for other in reversed(range(cores)):
                b = lax.rem(place // cores + d, ring) * cores + lax.rem(place + other, cores)
                to = g * nb + b
                if d == 0 and other == 0:
                    own = jnp.logical_and(to == w, r == g)

                    @pl.when(jnp.logical_not(own))
                    def _():
                        block_copy(b, (to, r)).start()

                    @pl.when(own)
                    def _():
                        local_copy(b).start()

                else:
                    block_copy(b, (to, r)).start()

    def send_blocks(r, distances):
        slot = recv.at[pl.ds(w * 2 * VEC, 2 * VEC)]
        to_owners(
            r,
            distances,
            lambda b, to: remote(fin.at[r, b], slot, fin_send.at[0], fin_recv.at[0], to),
            lambda b: pltpu.make_async_copy(fin.at[r, b], slot, fin_recv.at[0]),
        )

    gram_all[...] = jnp.zeros_like(gram_all)

    def last(rows):
        for r in rows:
            send_blocks(r, far)
        for r in rows:
            both = both_last[r]
            gram_all[...] += lax.dot_general(both, both, (((1,), (1,)), ((), ())), preferred_element_type=F32)

    for r in range(3):
        take_halos(DEG - 1, r)
    apply(DEG - 1, [(r, q) for r in (0, 1) for q in range(2)])
    last((0, 1))
    take_halos(DEG - 1, 3)
    apply(DEG - 1, [(r, q) for r in (2, 3) for q in range(2)])
    last((2, 3))

    states_gram = (gram_all[:chunk, chunk:] + gram_all[chunk:, :chunk] + gram_all[chunk:, chunk:]) + gram_all[:chunk, :chunk]
    row_id = lax.broadcasted_iota(jnp.int32, (chunk, chunk), 0)
    lane_id = lax.broadcasted_iota(jnp.int32, (chunk, chunk), 1)
    states_gram = jnp.where(row_id // VEC == lane_id // VEC, states_gram, 0.0)
    fold_row = lax.broadcasted_iota(jnp.int32, (chunk, BS), 0)
    fold_lane = lax.broadcasted_iota(jnp.int32, (chunk, BS), 1)
    fold = jnp.where(fold_row % VEC == fold_lane % VEC, 1.0, 0.0).astype(F32)
    folded = jnp.dot(states_gram, fold, precision=lax.Precision.HIGHEST, preferred_element_type=F32)
    folded = jnp.where(fold_row % VEC == fold_lane // VEC, folded, 0.0)
    flat = jnp.sum(folded.reshape(nb, VEC, BS), axis=1)
    for b in range(nb):
        gram_out[b] = flat[b : b + 1, :]

    @pl.loop(0, G)
    def _(d):
        r = row_at(d)
        to_owners(
            r,
            offsets,
            lambda b, to: remote(gram_out.at[b], gram_in.at[w], gram_send.at[0], gram_recv.at[0], to),
            lambda b: pltpu.make_async_copy(gram_out.at[b], gram_in.at[w], gram_recv.at[0]),
        )

    @pl.loop(0, G)
    def _(r):
        send_blocks(r, near)

    arrived(gram_in, gram_recv.at[0])
    whole = jnp.sum(gram_in[...], axis=0) * (1.0 / nodes)

    entry = {}
    for a in range(VEC):
        for c in range(a + 1):
            i = a * VEC + c
            entry[a, c] = jnp.broadcast_to(whole[:, i : i + 1], (VEC, BS))
    groups = 2 * wide // VEC

    def tiles(group):
        return [recv[pl.ds(group * VEC * VEC + s, VEC, stride=VEC), :] for s in range(VEC)]

    lower, inverse = {}, []
    for j in range(VEC):
        rest = entry[j, j]
        for k in range(j):
            rest = rest - lower[j, k] * lower[j, k]
        root = lax.rsqrt(rest)
        root = root * (1.5 - 0.5 * rest * root * root)
        inverse.append(root)
        for i in range(j + 1, VEC):
            value = entry[i, j]
            for k in range(j):
                value = value - lower[i, k] * lower[j, k]
            lower[i, j] = value * root
    for a in range(VEC):
        row = {}
        for c in reversed(range(VEC)):
            value = rot_wide[c * VEC + a]
            for k in range(c + 1, VEC):
                value = value - row[k] * lower[k, c]
            row[c] = value * inverse[c]
            mixer[a * VEC + c] = row[c]

    arrived(recv, fin_recv.at[0])

    @pl.loop(0, groups)
    def _(group):
        x = tiles(group)
        for a in range(VEC):
            value = mixer[a * VEC] * x[0]
            for c in range(1, VEC):
                value = value + mixer[a * VEC + c] * x[c]
            out[a, 0, pl.ds(pl.multiple_of(group * VEC, VEC), VEC), :] = value

    for d in range(1, G):
        slab_copy(d).wait_send()
        codes_copy(d).wait_send()
    for half in range(2):
        h_copy(half, 1).wait_send()
        h_copy(half, 3).wait_send()
    h_forward(first).wait_send()
    h_forward(other).wait_send()

    @pl.loop(0, DEG)
    def _(n):
        @pl.loop(0, G)
        def _(r):
            @pl.when(has_left)
            def _():
                halo_copy(n, r, 0).wait_send()

            @pl.when(has_right)
            def _():
                halo_copy(n, r, 1).wait_send()

    @pl.when(is_own)
    def _():
        part = recv.at[pl.ds(0, (wide - 1) * 2 * VEC)]
        arrived(part, fin_send.at[0])
        part = gram_in.at[pl.ds(0, wide - 1)]
        arrived(part, gram_send.at[0])

    @pl.when(jnp.logical_not(is_own))
    def _():
        arrived(recv, fin_send.at[0])
        arrived(gram_in, gram_send.at[0])


def body(slab, hblocks, blist, rotation):
    wide = lax.axis_size("wide")
    states = slab.shape[0]
    chunk = states // G
    nb = wide // G
    nodes = G * 2 * wide * BS
    dma = pltpu.SemaphoreType.DMA
    any_space = pl.BlockSpec(memory_space=pltpu.HBM)
    operands = (slab.reshape(2 * states, BS), hblocks.reshape(2, K, BS, BS), blist, jnp.transpose(rotation, (1, 2, 0)))
    operands = [pltpu.with_memory_space_constraint(value, pltpu.HBM) for value in operands]
    return pl.pallas_call(
        functools.partial(kernel, wide, nodes),
        out_shape=jax.ShapeDtypeStruct((VEC, 1, 2 * wide, BS), F32),
        in_specs=[any_space, any_space, any_space, any_space],
        out_specs=pl.BlockSpec(memory_space=pltpu.VMEM),
        scratch_shapes=[
            pltpu.VMEM((G, 2 * chunk, BS), F32),
            pltpu.VMEM((G, 2, K, BS, BS), F32),
            pltpu.VMEM((G, 2, K), jnp.int32),
            pltpu.SMEM((G, 2, K), jnp.int32),
            pltpu.SMEM((G, 16), jnp.int32),
            pltpu.VMEM((G, 2, 2 * BS, K * BS), BF16),
            pltpu.VMEM((DEG, G, 2, chunk, BS), F32),
            pltpu.VMEM((DEG, G, 2, chunk, BS), F32),
            pltpu.VMEM((DEG, 24, 2 * chunk, BS), BF16),
            pltpu.VMEM((G, nb, 2 * VEC, BS), F32),
            pltpu.VMEM((wide * 2 * VEC, BS), F32),
            pltpu.VMEM((G, 2 * chunk, 2 * BS), BF16),
            pltpu.VMEM((2 * chunk, 2 * chunk), F32),
            pltpu.VMEM((nb, 1, BS), F32),
            pltpu.VMEM((wide, 1, BS), F32),
            pltpu.VMEM((VEC, VEC, wide), F32),
            pltpu.VMEM((VEC * VEC, VEC, BS), F32),
            pltpu.VMEM((VEC * VEC, VEC, BS), F32),
            dma((5,)),
            dma((G,)),
            dma((G,)),
            dma((G,)),
            dma((G,)),
            dma((2, 3)),
            dma((G, 2)),
            dma((DEG, G, 2)),
            dma((DEG, G, 2)),
            dma((1,)),
            dma((1,)),
            dma((1,)),
            dma((1,)),
            pltpu.SemaphoreType.REGULAR((max(1, len(reach_steps(wide))),)),
        ],
        compiler_params=pltpu.CompilerParams(
            collective_id=0, has_side_effects=True, vmem_limit_bytes=40 * 1024 * 1024
        ),
        cost_estimate=pl.CostEstimate(flops=3 * 10**9, bytes_accessed=2 * 1024 * 1024, transcendentals=0),
    )(*operands)


def solution(mesh):
    in_specs = (
        P(None, "grp", "wide", None),
        P("grp", "wide", None, None, None),
        P("grp", "wide", None),
        P(),
    )
    out_specs = P("wide", "grp", None, None)
    return jax.shard_map(body, mesh=mesh, in_specs=in_specs, out_specs=out_specs, check_vma=False)
```

```python
import functools

import jax
import jax.numpy as jnp
from jax import lax
from jax.experimental import pallas as pl
from jax.experimental.pallas import tpu as pltpu
from jax.sharding import PartitionSpec as P

MESH = pl.DeviceIdType.MESH
F32 = jnp.float32
BF16 = jnp.bfloat16
VEC = 8
DEG = 4
BS = 128
K = 5
G = 4


def split(value):
    high = value.astype(BF16)
    low = (value - high.astype(F32)).astype(BF16)
    return high, low


def reach_steps(wide):
    steps, reach = [], 1
    while 2 * reach < wide:
        steps.append(reach)
        reach *= 2
    return steps


def kernel(
    wide,
    nodes,
    slab,
    hblocks,
    blist,
    rotation,
    out,
    slab_in,
    h_in,
    codes_in,
    codes_sm,
    position_sm,
    hs,
    fields,
    halo,
    xs,
    fin,
    recv,
    both_last,
    gram_all,
    gram_out,
    gram_in,
    rot_in,
    rot_wide,
    mixer,
    local_sem,
    slab_send,
    slab_recv,
    codes_send,
    codes_recv,
    h_send,
    h_recv,
    halo_send,
    halo_recv,
    fin_send,
    fin_recv,
    gram_send,
    gram_recv,
    reach_sem,
):
    w = lax.axis_index("wide")
    g = lax.axis_index("grp")
    nb = wide // G
    chunk = VEC * nb
    steps = reach_steps(wide)
    source = w // nb
    is_own = source == g
    has_left = w > 0
    has_right = w < wide - 1
    first = lax.rem(w, 2)
    other = 1 - first

    def remote(src, dst, send_sem, recv_sem, to):
        return pltpu.make_async_remote_copy(
            src_ref=src, dst_ref=dst, send_sem=send_sem, recv_sem=recv_sem, device_id=to, device_id_type=MESH
        )

    def arrived(ref, sem):
        pltpu.make_async_copy(ref, ref, sem).wait()

    def row_at(d):
        return lax.rem(g + d, G)

    def at_offset(d):
        return lax.rem(w + d, wide)

    barrier = pltpu.get_barrier_semaphore()
    for d in range(1, G):
        pl.semaphore_signal(barrier, inc=1, device_id=(w, row_at(d)), device_id_type=MESH)

    for to in (at_offset(1), at_offset(wide - 1)):
        pl.semaphore_signal(barrier, inc=1, device_id=(to, g), device_id_type=MESH)

    own_slab = pltpu.make_async_copy(slab.at[pl.ds(g * 2 * chunk, 2 * chunk)], slab_in.at[g], local_sem.at[0])
    own_slab.start()
    own_h = pltpu.make_async_copy(hblocks, h_in.at[g], local_sem.at[1])
    own_h.start()
    own_codes = pltpu.make_async_copy(blist.at[0], codes_in.at[g], local_sem.at[2])
    own_codes.start()
    own_rot = pltpu.make_async_copy(rotation, rot_in, local_sem.at[3])
    own_rot.start()

    zero = jnp.zeros((2 * chunk, BS), BF16)
    for n in range(DEG):
        for col in range(4):
            xs[n, col] = zero
            xs[n, 20 + col] = zero

        @pl.when(jnp.logical_not(has_left))
        def _():
            for r in range(G):
                xs[n, (r + 1) * 4] = zero

        @pl.when(jnp.logical_not(has_right))
        def _():
            for r in range(G):
                xs[n, (r + 1) * 4 + 3] = zero

    pl.semaphore_wait(barrier, G + 1)

    def greet(i):
        for to in (at_offset(steps[i]), at_offset(wide - steps[i])):
            pl.semaphore_signal(reach_sem.at[i], inc=1, device_id=(to, g), device_id_type=MESH)

    def greeted(i):
        pl.semaphore_wait(reach_sem.at[i], 2)
        if i + 1 < len(steps):
            greet(i + 1)

    greet(0)

    def slab_copy(d):
        to = row_at(d)
        return remote(
            slab.at[pl.ds(to * 2 * chunk, 2 * chunk)], slab_in.at[g], slab_send.at[d], slab_recv.at[g], (w, to)
        )

    def codes_copy(d):
        return remote(blist.at[0], codes_in.at[g], codes_send.at[d], codes_recv.at[g], (w, row_at(d)))

    def h_copy(half, d):
        return remote(
            hblocks.at[half], h_in.at[g, half], h_send.at[half, d // 2], h_recv.at[g, half], (w, row_at(d))
        )

    def h_forward(half):
        d = 1 + 2 * half
        origin = row_at(G - d)
        block = h_in.at[origin, half]
        return remote(block, block, h_send.at[half, 2], h_recv.at[origin, half], (w, row_at(d)))

    for d in (1, 3, 2):
        slab_copy(d).start()
    for d in (1, 3, 2):
        codes_copy(d).start()
    h_copy(first, 1 + 2 * first).start()
    h_copy(first, 3 - 2 * first).start()
    h_copy(other, 1 + 2 * other).start()
    h_copy(other, 3 - 2 * other).start()

    def split_column(r, q):
        for k in range(K):
            high, low = split(h_in[r, q, k])
            hs[r, q, 0:BS, k * BS : (k + 1) * BS] = high
            hs[r, q, BS : 2 * BS, k * BS : (k + 1) * BS] = low

    def split_h(r):
        for q in range(2):
            split_column(r, q)

    def store_split(n, position, value):
        high, low = split(value)
        xs[n, position, 0:chunk] = high
        xs[n, position, chunk : 2 * chunk] = low

    def halo_copy(n, r, side):
        return remote(
            fields.at[n, r, side],
            halo.at[n, r, 1 - side],
            halo_send.at[n, r, side],
            halo_recv.at[n, r, 1 - side],
            (w - 1 + 2 * side, g),
        )

    def send_halo(n, r, side):
        to = w - 1 + 2 * side

        @pl.when(jnp.logical_and(to >= 0, to < wide))
        def _():
            halo_copy(n, r, side).start()

    def take_halos(n, r):
        @pl.when(has_left)
        def _():
            halo_copy(n, r, 1).wait_recv()
            store_split(n, (r + 1) * 4, halo[n, r, 0])

        @pl.when(has_right)
        def _():
            halo_copy(n, r, 0).wait_recv()
            store_split(n, (r + 1) * 4 + 3, halo[n, r, 1])

    def product(n, r, q):
        picked = [xs[n, r * 4 + position_sm[r, q * 8 + k]] for k in range(K)]
        both = jnp.concatenate(picked, axis=1)
        p = lax.dot_general(both, hs[r, q], (((1,), (1,)), ((), ())), preferred_element_type=F32)
        small = p[:chunk, BS:] + p[chunk:, :BS] + p[chunk:, BS:]
        return p[:chunk, :BS] + small

    def apply(n, blocks):
        values = []
        for r, q in blocks:
            value = product(n, r, q)
            values.append(2.0 * value - fields[n - 1, r, q] if n > 0 else value)
        for (r, q), value in zip(blocks, values):
            if n + 1 < DEG:
                fields[n + 1, r, q] = value
                store_split(n + 1, (r + 1) * 4 + 1 + q, value)
            else:
                fin[r, :, q * VEC : (q + 1) * VEC, :] = value.reshape(nb, VEC, BS)
                high, low = split(value)
                both_last[r, 0:chunk, q * BS : (q + 1) * BS] = high
                both_last[r, chunk : 2 * chunk, q * BS : (q + 1) * BS] = low
        if n + 1 < DEG:
            for r, q in blocks:
                send_halo(n + 1, r, q)

    own_h.wait()
    split_h(g)
    own_rot.wait()
    mine = lax.broadcasted_iota(jnp.int32, (VEC, wide), 1) == w
    for c in range(VEC):
        column = jnp.sum(jnp.where(mine, rot_in[c], 0.0), axis=1, keepdims=True)
        for a in range(VEC):
            rot_wide[c * VEC + a] = jnp.broadcast_to(column[a : a + 1, :], (VEC, BS))

    def start_row(r):
        for q in range(2):
            value = slab_in[r, pl.ds(q, chunk, stride=2), :]
            fields[0, r, q] = value
            store_split(0, (r + 1) * 4 + 1 + q, value)
        send_halo(0, r, first)
        send_halo(0, r, other)

    own_slab.wait()
    start_row(g)
    for d in (1, 3, 2):
        arrived(slab_in.at[row_at(d)], slab_recv.at[row_at(d)])
        start_row(row_at(d))

    own_codes.wait()
    for d in (1, 3, 2):
        arrived(codes_in.at[row_at(d)], codes_recv.at[row_at(d)])
    to_scalars = pltpu.make_async_copy(codes_in, codes_sm, local_sem.at[4])
    to_scalars.start()
    to_scalars.wait()
    for r in range(G):
        for q in range(2):
            for k in range(K):
                code = codes_sm[r, q, k]
                line = (code * 11) >> 5
                position_sm[r, q * 8 + k] = line * 4 + code - 3 * line + q

    def h_wait(d, half):
        r = row_at(d)
        arrived(h_in.at[r, half], h_recv.at[r, half])

    waiting = list(range(len(steps)))

    def next_round():
        if waiting:
            greeted(waiting.pop(0))

    next_round()

    @pl.loop(0, G)
    def _(r):
        take_halos(0, r)

    apply(0, [(g, first), (g, other)])
    next_round()

    def take_h(d, q, forward):
        h_wait(d, q)
        if forward:
            h_forward(q).start()
        split_column(row_at(d), q)
        apply(0, [(row_at(d), q)])

    take_h(G - 1 - 2 * first, first, True)
    next_round()
    take_h(1 + 2 * first, first, False)
    next_round()
    take_h(1 + 2 * first, other, True)
    next_round()
    take_h(G - 1 - 2 * first, other, False)
    while waiting:
        next_round()
    take_h(2, first, False)
    for d in (0, 3, 1):
        take_halos(1, row_at(d))
    apply(1, [(g, first), (g, other)])
    take_h(2, other, False)

    take_halos(1, row_at(2))
    for q in (first, other):
        apply(1, [(row_at(d), q) for d in (3, 1, 2)])

    for r in range(3):
        take_halos(2, r)
    apply(2, [(0, first), (1, first)])
    take_halos(2, 3)
    apply(2, [(2, first), (3, first)])
    apply(2, [(r, other) for r in range(G)])

    cores = min(2, nb)
    ring = nb // cores
    offsets = sorted(range(ring), key=lambda d: -min(d, ring - d))
    far = [d for d in offsets if min(d, ring - d) > 1]
    near = [d for d in offsets if min(d, ring - d) <= 1]

    def to_owners(r, distances, block_copy, local_copy):
        place = lax.rem(w, nb)
        for d in distances:
            for other in reversed(range(cores)):
                b = lax.rem(place // cores + d, ring) * cores + lax.rem(place + other, cores)
                to = g * nb + b
                if d == 0 and other == 0:
                    own = jnp.logical_and(to == w, r == g)

                    @pl.when(jnp.logical_not(own))
                    def _():
                        block_copy(b, (to, r)).start()

                    @pl.when(own)
                    def _():
                        local_copy(b).start()

                else:
                    block_copy(b, (to, r)).start()

    def send_blocks(r, distances):
        slot = recv.at[pl.ds(w * 2 * VEC, 2 * VEC)]
        to_owners(
            r,
            distances,
            lambda b, to: remote(fin.at[r, b], slot, fin_send.at[0], fin_recv.at[0], to),
            lambda b: pltpu.make_async_copy(fin.at[r, b], slot, fin_recv.at[0]),
        )

    gram_all[...] = jnp.zeros_like(gram_all)

    def last(rows):
        for r in rows:
            send_blocks(r, far)
        for r in rows:
            both = both_last[r]
            gram_all[...] += lax.dot_general(both, both, (((1,), (1,)), ((), ())), preferred_element_type=F32)

    for r in range(3):
        take_halos(DEG - 1, r)
    apply(DEG - 1, [(r, q) for r in (0, 1) for q in range(2)])
    last((0, 1))
    take_halos(DEG - 1, 3)
    apply(DEG - 1, [(r, q) for r in (2, 3) for q in range(2)])
    last((2, 3))

    states_gram = (gram_all[:chunk, chunk:] + gram_all[chunk:, :chunk] + gram_all[chunk:, chunk:]) + gram_all[:chunk, :chunk]
    row_id = lax.broadcasted_iota(jnp.int32, (chunk, chunk), 0)
    lane_id = lax.broadcasted_iota(jnp.int32, (chunk, chunk), 1)
    states_gram = jnp.where(row_id // VEC == lane_id // VEC, states_gram, 0.0)
    fold_row = lax.broadcasted_iota(jnp.int32, (chunk, BS), 0)
    fold_lane = lax.broadcasted_iota(jnp.int32, (chunk, BS), 1)
    fold = jnp.where(fold_row % VEC == fold_lane % VEC, 1.0, 0.0).astype(F32)
    folded = jnp.dot(states_gram, fold, precision=lax.Precision.HIGHEST, preferred_element_type=F32)
    folded = jnp.where(fold_row % VEC == fold_lane // VEC, folded, 0.0)
    flat = jnp.sum(folded.reshape(nb, VEC, BS), axis=1)
    for b in range(nb):
        gram_out[b] = flat[b : b + 1, :]

    @pl.loop(0, G)
    def _(d):
        r = row_at(d)
        to_owners(
            r,
            offsets,
            lambda b, to: remote(gram_out.at[b], gram_in.at[w], gram_send.at[0], gram_recv.at[0], to),
            lambda b: pltpu.make_async_copy(gram_out.at[b], gram_in.at[w], gram_recv.at[0]),
        )

    @pl.loop(0, G)
    def _(r):
        send_blocks(r, near)

    arrived(gram_in, gram_recv.at[0])
    whole = jnp.sum(gram_in[...], axis=0) * (1.0 / nodes)

    entry = {}
    for a in range(VEC):
        for c in range(a + 1):
            i = a * VEC + c
            entry[a, c] = jnp.broadcast_to(whole[:, i : i + 1], (VEC, BS))
    groups = 2 * wide // VEC

    def tiles(group):
        return [recv[pl.ds(group * VEC * VEC + s, VEC, stride=VEC), :] for s in range(VEC)]

    lower, inverse = {}, []
    for j in range(VEC):
        rest = entry[j, j]
        for k in range(j):
            rest = rest - lower[j, k] * lower[j, k]
        root = lax.rsqrt(rest)
        root = root * (1.5 - 0.5 * rest * root * root)
        inverse.append(root)
        for i in range(j + 1, VEC):
            value = entry[i, j]
            for k in range(j):
                value = value - lower[i, k] * lower[j, k]
            lower[i, j] = value * root
    for a in range(VEC):
        row = {}
        for c in reversed(range(VEC)):
            value = rot_wide[c * VEC + a]
            for k in range(c + 1, VEC):
                value = value - row[k] * lower[k, c]
            row[c] = value * inverse[c]
            mixer[a * VEC + c] = row[c]

    arrived(recv, fin_recv.at[0])

    @pl.loop(0, groups)
    def _(group):
        x = tiles(group)
        for a in range(VEC):
            value = mixer[a * VEC] * x[0]
            for c in range(1, VEC):
                value = value + mixer[a * VEC + c] * x[c]
            out[a, 0, pl.ds(pl.multiple_of(group * VEC, VEC), VEC), :] = value

    for d in range(1, G):
        slab_copy(d).wait_send()
        codes_copy(d).wait_send()
    for half in range(2):
        h_copy(half, 1).wait_send()
        h_copy(half, 3).wait_send()
    h_forward(first).wait_send()
    h_forward(other).wait_send()

    @pl.loop(0, DEG)
    def _(n):
        @pl.loop(0, G)
        def _(r):
            @pl.when(has_left)
            def _():
                halo_copy(n, r, 0).wait_send()

            @pl.when(has_right)
            def _():
                halo_copy(n, r, 1).wait_send()

    @pl.when(is_own)
    def _():
        part = recv.at[pl.ds(0, (wide - 1) * 2 * VEC)]
        arrived(part, fin_send.at[0])
        part = gram_in.at[pl.ds(0, wide - 1)]
        arrived(part, gram_send.at[0])

    @pl.when(jnp.logical_not(is_own))
    def _():
        arrived(recv, fin_send.at[0])
        arrived(gram_in, gram_send.at[0])


def body(slab, hblocks, blist, rotation):
    wide = lax.axis_size("wide")
    states = slab.shape[0]
    chunk = states // G
    nb = wide // G
    nodes = G * 2 * wide * BS
    dma = pltpu.SemaphoreType.DMA
    any_space = pl.BlockSpec(memory_space=pltpu.HBM)
    operands = (slab.reshape(2 * states, BS), hblocks.reshape(2, K, BS, BS), blist, jnp.transpose(rotation, (1, 2, 0)))
    operands = [pltpu.with_memory_space_constraint(value, pltpu.HBM) for value in operands]
    return pl.pallas_call(
        functools.partial(kernel, wide, nodes),
        out_shape=jax.ShapeDtypeStruct((VEC, 1, 2 * wide, BS), F32),
        in_specs=[any_space, any_space, any_space, any_space],
        out_specs=pl.BlockSpec(memory_space=pltpu.VMEM),
        scratch_shapes=[
            pltpu.VMEM((G, 2 * chunk, BS), F32),
            pltpu.VMEM((G, 2, K, BS, BS), F32),
            pltpu.VMEM((G, 2, K), jnp.int32),
            pltpu.SMEM((G, 2, K), jnp.int32),
            pltpu.SMEM((G, 16), jnp.int32),
            pltpu.VMEM((G, 2, 2 * BS, K * BS), BF16),
            pltpu.VMEM((DEG, G, 2, chunk, BS), F32),
            pltpu.VMEM((DEG, G, 2, chunk, BS), F32),
            pltpu.VMEM((DEG, 24, 2 * chunk, BS), BF16),
            pltpu.VMEM((G, nb, 2 * VEC, BS), F32),
            pltpu.VMEM((wide * 2 * VEC, BS), F32),
            pltpu.VMEM((G, 2 * chunk, 2 * BS), BF16),
            pltpu.VMEM((2 * chunk, 2 * chunk), F32),
            pltpu.VMEM((nb, 1, BS), F32),
            pltpu.VMEM((wide, 1, BS), F32),
            pltpu.VMEM((VEC, VEC, wide), F32),
            pltpu.VMEM((VEC * VEC, VEC, BS), F32),
            pltpu.VMEM((VEC * VEC, VEC, BS), F32),
            dma((5,)),
            dma((G,)),
            dma((G,)),
            dma((G,)),
            dma((G,)),
            dma((2, 3)),
            dma((G, 2)),
            dma((DEG, G, 2)),
            dma((DEG, G, 2)),
            dma((1,)),
            dma((1,)),
            dma((1,)),
            dma((1,)),
            pltpu.SemaphoreType.REGULAR((max(1, len(reach_steps(wide))),)),
        ],
        compiler_params=pltpu.CompilerParams(
            collective_id=0, has_side_effects=True, vmem_limit_bytes=40 * 1024 * 1024
        ),
        cost_estimate=pl.CostEstimate(flops=3 * 10**9, bytes_accessed=2 * 1024 * 1024, transcendentals=0),
    )(*operands)


def solution(mesh):
    in_specs = (
        P(None, "grp", "wide", None),
        P("grp", "wide", None, None, None),
        P("grp", "wide", None),
        P(),
    )
    out_specs = P("wide", "grp", None, None)
    return jax.shard_map(body, mesh=mesh, in_specs=in_specs, out_specs=out_specs, check_vma=False)
```

```python
import functools

import jax
import jax.numpy as jnp
from jax import lax
from jax.experimental import pallas as pl
from jax.experimental.pallas import tpu as pltpu
from jax.sharding import PartitionSpec as P

MESH = pl.DeviceIdType.MESH
F32 = jnp.float32
BF16 = jnp.bfloat16
VEC = 8
DEG = 4
BS = 128
K = 5
G = 4


def split(value):
    high = value.astype(BF16)
    low = (value - high.astype(F32)).astype(BF16)
    return high, low


def reach_steps(wide):
    steps, reach = [], 1
    while 2 * reach < wide:
        steps.append(reach)
        reach *= 2
    return steps


def kernel(
    wide,
    nodes,
    slab,
    hblocks,
    blist,
    rotation,
    out,
    slab_in,
    h_in,
    codes_in,
    codes_sm,
    position_sm,
    hs,
    fields,
    halo,
    xs,
    fin,
    recv,
    both_last,
    gram_all,
    gram_out,
    gram_in,
    rot_in,
    rot_wide,
    mixer,
    local_sem,
    slab_send,
    slab_recv,
    codes_send,
    codes_recv,
    h_send,
    h_recv,
    halo_send,
    halo_recv,
    fin_send,
    fin_recv,
    gram_send,
    gram_recv,
    reach_sem,
):
    w = lax.axis_index("wide")
    g = lax.axis_index("grp")
    nb = wide // G
    chunk = VEC * nb
    steps = reach_steps(wide)
    source = w // nb
    is_own = source == g
    has_left = w > 0
    has_right = w < wide - 1
    first = lax.rem(w, 2)
    other = 1 - first

    def remote(src, dst, send_sem, recv_sem, to):
        return pltpu.make_async_remote_copy(
            src_ref=src, dst_ref=dst, send_sem=send_sem, recv_sem=recv_sem, device_id=to, device_id_type=MESH
        )

    def arrived(ref, sem):
        pltpu.make_async_copy(ref, ref, sem).wait()

    def row_at(d):
        return lax.rem(g + d, G)

    def at_offset(d):
        return lax.rem(w + d, wide)

    barrier = pltpu.get_barrier_semaphore()
    for d in range(1, G):
        pl.semaphore_signal(barrier, inc=1, device_id=(w, row_at(d)), device_id_type=MESH)

    for to in (at_offset(1), at_offset(wide - 1)):
        pl.semaphore_signal(barrier, inc=1, device_id=(to, g), device_id_type=MESH)

    own_slab = pltpu.make_async_copy(slab.at[pl.ds(g * 2 * chunk, 2 * chunk)], slab_in.at[g], local_sem.at[0])
    own_slab.start()
    own_h = pltpu.make_async_copy(hblocks, h_in.at[g], local_sem.at[1])
    own_h.start()
    own_codes = pltpu.make_async_copy(blist.at[0], codes_in.at[g], local_sem.at[2])
    own_codes.start()
    own_rot = pltpu.make_async_copy(rotation, rot_in, local_sem.at[3])
    own_rot.start()

    zero = jnp.zeros((2 * chunk, BS), BF16)
    for n in range(DEG):
        for col in range(4):
            xs[n, col] = zero
            xs[n, 20 + col] = zero

        @pl.when(jnp.logical_not(has_left))
        def _():
            for r in range(G):
                xs[n, (r + 1) * 4] = zero

        @pl.when(jnp.logical_not(has_right))
        def _():
            for r in range(G):
                xs[n, (r + 1) * 4 + 3] = zero

    pl.semaphore_wait(barrier, G + 1)

    def greet(i):
        for to in (at_offset(steps[i]), at_offset(wide - steps[i])):
            pl.semaphore_signal(reach_sem.at[i], inc=1, device_id=(to, g), device_id_type=MESH)

    def greeted(i):
        pl.semaphore_wait(reach_sem.at[i], 2)
        if i + 1 < len(steps):
            greet(i + 1)

    greet(0)

    def slab_copy(d):
        to = row_at(d)
        return remote(
            slab.at[pl.ds(to * 2 * chunk, 2 * chunk)], slab_in.at[g], slab_send.at[d], slab_recv.at[g], (w, to)
        )

    def codes_copy(d):
        return remote(blist.at[0], codes_in.at[g], codes_send.at[d], codes_recv.at[g], (w, row_at(d)))

    def h_copy(half, d):
        return remote(
            hblocks.at[half], h_in.at[g, half], h_send.at[half, d // 2], h_recv.at[g, half], (w, row_at(d))
        )

    def h_forward(half):
        d = 1 + 2 * half
        origin = row_at(G - d)
        block = h_in.at[origin, half]
        return remote(block, block, h_send.at[half, 2], h_recv.at[origin, half], (w, row_at(d)))

    for d in (1, 3, 2):
        slab_copy(d).start()
    for d in (1, 3, 2):
        codes_copy(d).start()
    h_copy(first, 1 + 2 * first).start()
    h_copy(first, 3 - 2 * first).start()
    h_copy(other, 1 + 2 * other).start()
    h_copy(other, 3 - 2 * other).start()

    def split_column(r, q):
        for k in range(K):
            high, low = split(h_in[r, q, k].T)
            hs[r, q, k * BS : (k + 1) * BS, 0:BS] = high
            hs[r, q, k * BS : (k + 1) * BS, BS : 2 * BS] = low

    def split_h(r):
        for q in range(2):
            split_column(r, q)

    def store_split(n, position, value):
        high, low = split(value)
        xs[n, position, 0:chunk] = high
        xs[n, position, chunk : 2 * chunk] = low

    def halo_copy(n, r, side):
        return remote(
            fields.at[n, r, side],
            halo.at[n, r, 1 - side],
            halo_send.at[n, r, side],
            halo_recv.at[n, r, 1 - side],
            (w - 1 + 2 * side, g),
        )

    def send_halo(n, r, side):
        to = w - 1 + 2 * side

        @pl.when(jnp.logical_and(to >= 0, to < wide))
        def _():
            halo_copy(n, r, side).start()

    def take_halos(n, r):
        @pl.when(has_left)
        def _():
            halo_copy(n, r, 1).wait_recv()
            store_split(n, (r + 1) * 4, halo[n, r, 0])

        @pl.when(has_right)
        def _():
            halo_copy(n, r, 0).wait_recv()
            store_split(n, (r + 1) * 4 + 3, halo[n, r, 1])

    def product(n, r, q):
        picked = [xs[n, r * 4 + position_sm[r, q * 8 + k]] for k in range(K)]
        both = jnp.concatenate(picked, axis=1)
        p = jnp.dot(both, hs[r, q], preferred_element_type=F32)
        small = p[:chunk, BS:] + p[chunk:, :BS] + p[chunk:, BS:]
        return p[:chunk, :BS] + small

    def apply(n, blocks):
        values = []
        for r, q in blocks:
            value = product(n, r, q)
            values.append(2.0 * value - fields[n - 1, r, q] if n > 0 else value)
        for (r, q), value in zip(blocks, values):
            if n + 1 < DEG:
                fields[n + 1, r, q] = value
                store_split(n + 1, (r + 1) * 4 + 1 + q, value)
            else:
                fin[r, :, q * VEC : (q + 1) * VEC, :] = value.reshape(nb, VEC, BS)
                high, low = split(value)
                both_last[r, 0:chunk, q * BS : (q + 1) * BS] = high
                both_last[r, chunk : 2 * chunk, q * BS : (q + 1) * BS] = low
        if n + 1 < DEG:
            for r, q in blocks:
                send_halo(n + 1, r, q)

    own_h.wait()
    split_h(g)
    own_rot.wait()
    mine = lax.broadcasted_iota(jnp.int32, (VEC, wide), 1) == w
    for c in range(VEC):
        column = jnp.sum(jnp.where(mine, rot_in[c], 0.0), axis=1, keepdims=True)
        for a in range(VEC):
            rot_wide[c * VEC + a] = jnp.broadcast_to(column[a : a + 1, :], (VEC, BS))

    def start_row(r):
        for q in range(2):
            value = slab_in[r, pl.ds(q, chunk, stride=2), :]
            fields[0, r, q] = value
            store_split(0, (r + 1) * 4 + 1 + q, value)
        send_halo(0, r, first)
        send_halo(0, r, other)

    own_slab.wait()
    start_row(g)
    for d in (1, 3, 2):
        arrived(slab_in.at[row_at(d)], slab_recv.at[row_at(d)])
        start_row(row_at(d))

    own_codes.wait()
    for d in (1, 3, 2):
        arrived(codes_in.at[row_at(d)], codes_recv.at[row_at(d)])
    to_scalars = pltpu.make_async_copy(codes_in, codes_sm, local_sem.at[4])
    to_scalars.start()
    to_scalars.wait()
    for r in range(G):
        for q in range(2):
            for k in range(K):
                code = codes_sm[r, q, k]
                line = (code * 11) >> 5
                position_sm[r, q * 8 + k] = line * 4 + code - 3 * line + q

    def h_wait(d, half):
        r = row_at(d)
        arrived(h_in.at[r, half], h_recv.at[r, half])

    waiting = list(range(len(steps)))

    def next_round():
        if waiting:
            greeted(waiting.pop(0))

    next_round()

    h_wait(G - 1 - 2 * first, first)
    h_forward(first).start()

    @pl.loop(0, G)
    def _(r):
        take_halos(0, r)

    apply(0, [(g, first), (g, other)])
    next_round()

    def take_h(d, q, forward):
        h_wait(d, q)
        if forward:
            h_forward(q).start()
        split_column(row_at(d), q)
        apply(0, [(row_at(d), q)])

    split_column(row_at(G - 1 - 2 * first), first)
    apply(0, [(row_at(G - 1 - 2 * first), first)])
    next_round()
    take_h(1 + 2 * first, first, False)
    next_round()
    take_h(1 + 2 * first, other, True)
    next_round()
    take_h(G - 1 - 2 * first, other, False)
    while waiting:
        next_round()
    take_h(2, first, False)
    for d in (0, 3, 1):
        take_halos(1, row_at(d))
    apply(1, [(g, first), (g, other)])
    take_h(2, other, False)

    take_halos(1, row_at(2))
    for q in (first, other):
        apply(1, [(row_at(d), q) for d in (3, 1, 2)])

    for r in range(3):
        take_halos(2, r)
    apply(2, [(0, first), (1, first)])
    take_halos(2, 3)
    apply(2, [(2, first), (3, first)])
    apply(2, [(r, other) for r in range(G)])

    cores = min(2, nb)
    ring = nb // cores
    offsets = sorted(range(ring), key=lambda d: -min(d, ring - d))
    far = [d for d in offsets if min(d, ring - d) > 1]
    near = [d for d in offsets if min(d, ring - d) <= 1]

    def to_owners(r, distances, block_copy, local_copy):
        place = lax.rem(w, nb)
        for d in distances:
            for other in reversed(range(cores)):
                b = lax.rem(place // cores + d, ring) * cores + lax.rem(place + other, cores)
                to = g * nb + b
                if d == 0 and other == 0:
                    own = jnp.logical_and(to == w, r == g)

                    @pl.when(jnp.logical_not(own))
                    def _():
                        block_copy(b, (to, r)).start()

                    @pl.when(own)
                    def _():
                        local_copy(b).start()

                else:
                    block_copy(b, (to, r)).start()

    def send_blocks(r, distances):
        slot = recv.at[pl.ds(w * 2 * VEC, 2 * VEC)]
        to_owners(
            r,
            distances,
            lambda b, to: remote(fin.at[r, b], slot, fin_send.at[0], fin_recv.at[0], to),
            lambda b: pltpu.make_async_copy(fin.at[r, b], slot, fin_recv.at[0]),
        )

    gram_all[...] = jnp.zeros_like(gram_all)

    def last(rows):
        for r in rows:
            send_blocks(r, far)
        for r in rows:
            both = both_last[r]
            gram_all[...] += lax.dot_general(both, both, (((1,), (1,)), ((), ())), preferred_element_type=F32)

    for r in range(3):
        take_halos(DEG - 1, r)
    apply(DEG - 1, [(r, q) for r in (0, 1) for q in range(2)])
    last((0, 1))
    take_halos(DEG - 1, 3)
    apply(DEG - 1, [(r, q) for r in (2, 3) for q in range(2)])
    last((2, 3))

    states_gram = (gram_all[:chunk, chunk:] + gram_all[chunk:, :chunk] + gram_all[chunk:, chunk:]) + gram_all[:chunk, :chunk]
    row_id = lax.broadcasted_iota(jnp.int32, (chunk, chunk), 0)
    lane_id = lax.broadcasted_iota(jnp.int32, (chunk, chunk), 1)
    states_gram = jnp.where(row_id // VEC == lane_id // VEC, states_gram, 0.0)
    fold_row = lax.broadcasted_iota(jnp.int32, (chunk, BS), 0)
    fold_lane = lax.broadcasted_iota(jnp.int32, (chunk, BS), 1)
    fold = jnp.where(fold_row % VEC == fold_lane % VEC, 1.0, 0.0).astype(F32)
    folded = jnp.dot(states_gram, fold, precision=lax.Precision.HIGHEST, preferred_element_type=F32)
    folded = jnp.where(fold_row % VEC == fold_lane // VEC, folded, 0.0)
    flat = jnp.sum(folded.reshape(nb, VEC, BS), axis=1)
    for b in range(nb):
        gram_out[b] = flat[b : b + 1, :]

    @pl.loop(0, G)
    def _(d):
        r = row_at(d)
        to_owners(
            r,
            offsets,
            lambda b, to: remote(gram_out.at[b], gram_in.at[w], gram_send.at[0], gram_recv.at[0], to),
            lambda b: pltpu.make_async_copy(gram_out.at[b], gram_in.at[w], gram_recv.at[0]),
        )

    @pl.loop(0, G)
    def _(r):
        send_blocks(r, near)

    arrived(gram_in, gram_recv.at[0])
    whole = jnp.sum(gram_in[...], axis=0) * (1.0 / nodes)

    entry = {}
    for a in range(VEC):
        for c in range(a + 1):
            i = a * VEC + c
            entry[a, c] = jnp.broadcast_to(whole[:, i : i + 1], (VEC, BS))
    groups = 2 * wide // VEC

    def tiles(group):
        return [recv[pl.ds(group * VEC * VEC + s, VEC, stride=VEC), :] for s in range(VEC)]

    lower, inverse = {}, []
    for j in range(VEC):
        rest = entry[j, j]
        for k in range(j):
            rest = rest - lower[j, k] * lower[j, k]
        root = lax.rsqrt(rest)
        root = root * (1.5 - 0.5 * rest * root * root)
        inverse.append(root)
        for i in range(j + 1, VEC):
            value = entry[i, j]
            for k in range(j):
                value = value - lower[i, k] * lower[j, k]
            lower[i, j] = value * root
    for a in range(VEC):
        row = {}
        for c in reversed(range(VEC)):
            value = rot_wide[c * VEC + a]
            for k in range(c + 1, VEC):
                value = value - row[k] * lower[k, c]
            row[c] = value * inverse[c]
            mixer[a * VEC + c] = row[c]

    arrived(recv, fin_recv.at[0])

    @pl.loop(0, groups)
    def _(group):
        x = tiles(group)
        for a in range(VEC):
            value = mixer[a * VEC] * x[0]
            for c in range(1, VEC):
                value = value + mixer[a * VEC + c] * x[c]
            out[a, 0, pl.ds(pl.multiple_of(group * VEC, VEC), VEC), :] = value

    for d in range(1, G):
        slab_copy(d).wait_send()
        codes_copy(d).wait_send()
    for half in range(2):
        h_copy(half, 1).wait_send()
        h_copy(half, 3).wait_send()
    h_forward(first).wait_send()
    h_forward(other).wait_send()

    @pl.loop(0, DEG)
    def _(n):
        @pl.loop(0, G)
        def _(r):
            @pl.when(has_left)
            def _():
                halo_copy(n, r, 0).wait_send()

            @pl.when(has_right)
            def _():
                halo_copy(n, r, 1).wait_send()

    @pl.when(is_own)
    def _():
        part = recv.at[pl.ds(0, (wide - 1) * 2 * VEC)]
        arrived(part, fin_send.at[0])
        part = gram_in.at[pl.ds(0, wide - 1)]
        arrived(part, gram_send.at[0])

    @pl.when(jnp.logical_not(is_own))
    def _():
        arrived(recv, fin_send.at[0])
        arrived(gram_in, gram_send.at[0])


def body(slab, hblocks, blist, rotation):
    wide = lax.axis_size("wide")
    states = slab.shape[0]
    chunk = states // G
    nb = wide // G
    nodes = G * 2 * wide * BS
    dma = pltpu.SemaphoreType.DMA
    any_space = pl.BlockSpec(memory_space=pltpu.HBM)
    operands = (slab.reshape(2 * states, BS), hblocks.reshape(2, K, BS, BS), blist, jnp.transpose(rotation, (1, 2, 0)))
    operands = [pltpu.with_memory_space_constraint(value, pltpu.HBM) for value in operands]
    return pl.pallas_call(
        functools.partial(kernel, wide, nodes),
        out_shape=jax.ShapeDtypeStruct((VEC, 1, 2 * wide, BS), F32),
        in_specs=[any_space, any_space, any_space, any_space],
        out_specs=pl.BlockSpec(memory_space=pltpu.VMEM),
        scratch_shapes=[
            pltpu.VMEM((G, 2 * chunk, BS), F32),
            pltpu.VMEM((G, 2, K, BS, BS), F32),
            pltpu.VMEM((G, 2, K), jnp.int32),
            pltpu.SMEM((G, 2, K), jnp.int32),
            pltpu.SMEM((G, 16), jnp.int32),
            pltpu.VMEM((G, 2, K * BS, 2 * BS), BF16),
            pltpu.VMEM((DEG, G, 2, chunk, BS), F32),
            pltpu.VMEM((DEG, G, 2, chunk, BS), F32),
            pltpu.VMEM((DEG, 24, 2 * chunk, BS), BF16),
            pltpu.VMEM((G, nb, 2 * VEC, BS), F32),
            pltpu.VMEM((wide * 2 * VEC, BS), F32),
            pltpu.VMEM((G, 2 * chunk, 2 * BS), BF16),
            pltpu.VMEM((2 * chunk, 2 * chunk), F32),
            pltpu.VMEM((nb, 1, BS), F32),
            pltpu.VMEM((wide, 1, BS), F32),
            pltpu.VMEM((VEC, VEC, wide), F32),
            pltpu.VMEM((VEC * VEC, VEC, BS), F32),
            pltpu.VMEM((VEC * VEC, VEC, BS), F32),
            dma((5,)),
            dma((G,)),
            dma((G,)),
            dma((G,)),
            dma((G,)),
            dma((2, 3)),
            dma((G, 2)),
            dma((DEG, G, 2)),
            dma((DEG, G, 2)),
            dma((1,)),
            dma((1,)),
            dma((1,)),
            dma((1,)),
            pltpu.SemaphoreType.REGULAR((max(1, len(reach_steps(wide))),)),
        ],
        compiler_params=pltpu.CompilerParams(
            collective_id=0, has_side_effects=True, vmem_limit_bytes=40 * 1024 * 1024
        ),
        cost_estimate=pl.CostEstimate(flops=3 * 10**9, bytes_accessed=2 * 1024 * 1024, transcendentals=0),
    )(*operands)


def solution(mesh):
    in_specs = (
        P(None, "grp", "wide", None),
        P("grp", "wide", None, None, None),
        P("grp", "wide", None),
        P(),
    )
    out_specs = P("wide", "grp", None, None)
    return jax.shard_map(body, mesh=mesh, in_specs=in_specs, out_specs=out_specs, check_vma=False)
```

```python
import functools

import jax
import jax.numpy as jnp
from jax import lax
from jax.experimental import pallas as pl
from jax.experimental.pallas import tpu as pltpu
from jax.sharding import PartitionSpec as P

MESH = pl.DeviceIdType.MESH
F32 = jnp.float32
BF16 = jnp.bfloat16
VEC = 8
DEG = 4
BS = 128
K = 5
G = 4


def split(value):
    high = value.astype(BF16)
    low = (value - high.astype(F32)).astype(BF16)
    return high, low


def reach_steps(wide):
    steps, reach = [], 1
    while 2 * reach < wide:
        steps.append(reach)
        reach *= 2
    return steps


def kernel(
    wide,
    nodes,
    slab,
    hblocks,
    blist,
    rotation,
    out,
    slab_in,
    h_in,
    codes_in,
    codes_sm,
    position_sm,
    hs,
    fields,
    halo,
    xs,
    fin,
    recv,
    both_last,
    gram_all,
    gram_out,
    gram_in,
    rot_in,
    rot_wide,
    mixer,
    local_sem,
    slab_send,
    slab_recv,
    codes_send,
    codes_recv,
    h_send,
    h_recv,
    halo_send,
    halo_recv,
    fin_send,
    fin_recv,
    gram_send,
    gram_recv,
    reach_sem,
):
    w = lax.axis_index("wide")
    g = lax.axis_index("grp")
    nb = wide // G
    chunk = VEC * nb
    steps = reach_steps(wide)
    source = w // nb
    is_own = source == g
    has_left = w > 0
    has_right = w < wide - 1
    first = lax.rem(w, 2)
    other = 1 - first

    def remote(src, dst, send_sem, recv_sem, to):
        return pltpu.make_async_remote_copy(
            src_ref=src, dst_ref=dst, send_sem=send_sem, recv_sem=recv_sem, device_id=to, device_id_type=MESH
        )

    def arrived(ref, sem):
        pltpu.make_async_copy(ref, ref, sem).wait()

    def row_at(d):
        return lax.rem(g + d, G)

    def at_offset(d):
        return lax.rem(w + d, wide)

    barrier = pltpu.get_barrier_semaphore()
    for d in range(1, G):
        pl.semaphore_signal(barrier, inc=1, device_id=(w, row_at(d)), device_id_type=MESH)

    for to in (at_offset(1), at_offset(wide - 1)):
        pl.semaphore_signal(barrier, inc=1, device_id=(to, g), device_id_type=MESH)

    own_slab = pltpu.make_async_copy(slab.at[pl.ds(g * 2 * chunk, 2 * chunk)], slab_in.at[g], local_sem.at[0])
    own_slab.start()
    own_h = pltpu.make_async_copy(hblocks, h_in.at[g], local_sem.at[1])
    own_h.start()
    own_codes = pltpu.make_async_copy(blist.at[0], codes_in.at[g], local_sem.at[2])
    own_codes.start()
    own_rot = pltpu.make_async_copy(rotation, rot_in, local_sem.at[3])
    own_rot.start()

    zero = jnp.zeros((2 * chunk, BS), BF16)
    for n in range(DEG):
        for col in range(4):
            xs[n, col] = zero
            xs[n, 20 + col] = zero

        @pl.when(jnp.logical_not(has_left))
        def _():
            for r in range(G):
                xs[n, (r + 1) * 4] = zero

        @pl.when(jnp.logical_not(has_right))
        def _():
            for r in range(G):
                xs[n, (r + 1) * 4 + 3] = zero

    pl.semaphore_wait(barrier, G + 1)

    def greet(i):
        for to in (at_offset(steps[i]), at_offset(wide - steps[i])):
            pl.semaphore_signal(reach_sem.at[i], inc=1, device_id=(to, g), device_id_type=MESH)

    def greeted(i):
        pl.semaphore_wait(reach_sem.at[i], 2)
        if i + 1 < len(steps):
            greet(i + 1)

    greet(0)

    def slab_copy(d):
        to = row_at(d)
        return remote(
            slab.at[pl.ds(to * 2 * chunk, 2 * chunk)], slab_in.at[g], slab_send.at[d], slab_recv.at[g], (w, to)
        )

    def codes_copy(d):
        return remote(blist.at[0], codes_in.at[g], codes_send.at[d], codes_recv.at[g], (w, row_at(d)))

    def h_copy(half, d):
        return remote(
            hblocks.at[half], h_in.at[g, half], h_send.at[half, d // 2], h_recv.at[g, half], (w, row_at(d))
        )

    def h_forward(half):
        d = 1 + 2 * half
        origin = row_at(G - d)
        block = h_in.at[origin, half]
        return remote(block, block, h_send.at[half, 2], h_recv.at[origin, half], (w, row_at(d)))

    for d in (1, 3, 2):
        slab_copy(d).start()
    for d in (1, 3, 2):
        codes_copy(d).start()
    h_copy(first, 1 + 2 * first).start()
    h_copy(first, 3 - 2 * first).start()
    h_copy(other, 1 + 2 * other).start()
    h_copy(other, 3 - 2 * other).start()

    def split_column(r, q):
        for k in range(K):
            high, low = split(h_in[r, q, k].T)
            hs[r, q, k * BS : (k + 1) * BS, 0:BS] = high
            hs[r, q, k * BS : (k + 1) * BS, BS : 2 * BS] = low

    def split_h(r):
        for q in range(2):
            split_column(r, q)

    def store_split(n, position, value):
        high, low = split(value)
        xs[n, position, 0:chunk] = high
        xs[n, position, chunk : 2 * chunk] = low

    def halo_copy(n, r, side):
        return remote(
            fields.at[n, r, side],
            halo.at[n, r, 1 - side],
            halo_send.at[n, r, side],
            halo_recv.at[n, r, 1 - side],
            (w - 1 + 2 * side, g),
        )

    def send_halo(n, r, side):
        to = w - 1 + 2 * side

        @pl.when(jnp.logical_and(to >= 0, to < wide))
        def _():
            halo_copy(n, r, side).start()

    def take_halos(n, r):
        @pl.when(has_left)
        def _():
            halo_copy(n, r, 1).wait_recv()
            store_split(n, (r + 1) * 4, halo[n, r, 0])

        @pl.when(has_right)
        def _():
            halo_copy(n, r, 0).wait_recv()
            store_split(n, (r + 1) * 4 + 3, halo[n, r, 1])

    def product(n, r, q):
        picked = [xs[n, r * 4 + position_sm[r, q * 8 + k]] for k in range(K)]
        both = jnp.concatenate(picked, axis=1)
        p = jnp.dot(both, hs[r, q], preferred_element_type=F32)
        small = p[:chunk, BS:] + p[chunk:, :BS] + p[chunk:, BS:]
        return p[:chunk, :BS] + small

    def apply(n, blocks):
        values = []
        for r, q in blocks:
            value = product(n, r, q)
            values.append(2.0 * value - fields[n - 1, r, q] if n > 0 else value)
        for (r, q), value in zip(blocks, values):
            if n + 1 < DEG:
                fields[n + 1, r, q] = value
                store_split(n + 1, (r + 1) * 4 + 1 + q, value)
            else:
                fin[r, :, q * VEC : (q + 1) * VEC, :] = value.reshape(nb, VEC, BS)
                high, low = split(value)
                both_last[r, 0:chunk, q * BS : (q + 1) * BS] = high
                both_last[r, chunk : 2 * chunk, q * BS : (q + 1) * BS] = low
        if n + 1 < DEG:
            for r, q in blocks:
                send_halo(n + 1, r, q)

    own_h.wait()
    split_h(g)
    own_rot.wait()
    mine = lax.broadcasted_iota(jnp.int32, (VEC, wide), 1) == w
    for c in range(VEC):
        column = jnp.sum(jnp.where(mine, rot_in[c], 0.0), axis=1, keepdims=True)
        for a in range(VEC):
            rot_wide[c * VEC + a] = jnp.broadcast_to(column[a : a + 1, :], (VEC, BS))

    def start_row(r):
        for q in range(2):
            value = slab_in[r, pl.ds(q, chunk, stride=2), :]
            fields[0, r, q] = value
            store_split(0, (r + 1) * 4 + 1 + q, value)
        send_halo(0, r, first)
        send_halo(0, r, other)

    own_slab.wait()
    start_row(g)
    for d in (1, 3, 2):
        arrived(slab_in.at[row_at(d)], slab_recv.at[row_at(d)])
        start_row(row_at(d))

    own_codes.wait()
    for d in (1, 3, 2):
        arrived(codes_in.at[row_at(d)], codes_recv.at[row_at(d)])
    to_scalars = pltpu.make_async_copy(codes_in, codes_sm, local_sem.at[4])
    to_scalars.start()
    to_scalars.wait()
    for r in range(G):
        for q in range(2):
            for k in range(K):
                code = codes_sm[r, q, k]
                line = (code * 11) >> 5
                position_sm[r, q * 8 + k] = line * 4 + code - 3 * line + q

    def h_wait(d, half):
        r = row_at(d)
        arrived(h_in.at[r, half], h_recv.at[r, half])

    waiting = list(range(len(steps)))

    def next_round():
        if waiting:
            greeted(waiting.pop(0))

    next_round()

    h_wait(G - 1 - 2 * first, first)
    h_forward(first).start()

    @pl.loop(0, G)
    def _(r):
        take_halos(0, r)

    apply(0, [(g, first), (g, other)])
    next_round()

    def take_h(d, q, forward):
        h_wait(d, q)
        if forward:
            h_forward(q).start()
        split_column(row_at(d), q)
        apply(0, [(row_at(d), q)])

    split_column(row_at(G - 1 - 2 * first), first)
    apply(0, [(row_at(G - 1 - 2 * first), first)])
    next_round()
    take_h(1 + 2 * first, first, False)
    next_round()
    take_h(1 + 2 * first, other, True)
    next_round()
    take_h(G - 1 - 2 * first, other, False)
    while waiting:
        next_round()
    take_h(2, first, False)
    for d in (0, 3, 1):
        take_halos(1, row_at(d))
    apply(1, [(g, first), (g, other)])
    take_h(2, other, False)

    take_halos(1, row_at(2))
    for q in (first, other):
        apply(1, [(row_at(d), q) for d in (3, 1, 2)])

    for r in range(3):
        take_halos(2, r)
    apply(2, [(0, first)])
    apply(2, [(1, first)])
    take_halos(2, 3)
    apply(2, [(2, first), (3, first)])
    apply(2, [(r, other) for r in range(G)])

    cores = min(2, nb)
    ring = nb // cores
    offsets = sorted(range(ring), key=lambda d: -min(d, ring - d))
    far = [d for d in offsets if min(d, ring - d) > 1]
    near = [d for d in offsets if min(d, ring - d) <= 1]

    def to_owners(r, distances, block_copy, local_copy):
        place = lax.rem(w, nb)
        for d in distances:
            for other in reversed(range(cores)):
                b = lax.rem(place // cores + d, ring) * cores + lax.rem(place + other, cores)
                to = g * nb + b
                if d == 0 and other == 0:
                    own = jnp.logical_and(to == w, r == g)

                    @pl.when(jnp.logical_not(own))
                    def _():
                        block_copy(b, (to, r)).start()

                    @pl.when(own)
                    def _():
                        local_copy(b).start()

                else:
                    block_copy(b, (to, r)).start()

    def send_blocks(r, distances):
        slot = recv.at[pl.ds(w * 2 * VEC, 2 * VEC)]
        to_owners(
            r,
            distances,
            lambda b, to: remote(fin.at[r, b], slot, fin_send.at[0], fin_recv.at[0], to),
            lambda b: pltpu.make_async_copy(fin.at[r, b], slot, fin_recv.at[0]),
        )

    gram_all[...] = jnp.zeros_like(gram_all)

    def last(rows):
        for r in rows:
            send_blocks(r, far)
        for r in rows:
            both = both_last[r]
            gram_all[...] += lax.dot_general(both, both, (((1,), (1,)), ((), ())), preferred_element_type=F32)

    for r in range(3):
        take_halos(DEG - 1, r)
    for r in (0, 1):
        apply(DEG - 1, [(r, 0), (r, 1)])
        last((r,))
    take_halos(DEG - 1, 3)
    apply(DEG - 1, [(r, q) for r in (2, 3) for q in range(2)])
    last((2, 3))

    states_gram = (gram_all[:chunk, chunk:] + gram_all[chunk:, :chunk] + gram_all[chunk:, chunk:]) + gram_all[:chunk, :chunk]
    row_id = lax.broadcasted_iota(jnp.int32, (chunk, chunk), 0)
    lane_id = lax.broadcasted_iota(jnp.int32, (chunk, chunk), 1)
    states_gram = jnp.where(row_id // VEC == lane_id // VEC, states_gram, 0.0)
    fold_row = lax.broadcasted_iota(jnp.int32, (chunk, BS), 0)
    fold_lane = lax.broadcasted_iota(jnp.int32, (chunk, BS), 1)
    fold = jnp.where(fold_row % VEC == fold_lane % VEC, 1.0, 0.0).astype(F32)
    folded = jnp.dot(states_gram, fold, precision=lax.Precision.HIGHEST, preferred_element_type=F32)
    folded = jnp.where(fold_row % VEC == fold_lane // VEC, folded, 0.0)
    flat = jnp.sum(folded.reshape(nb, VEC, BS), axis=1)
    for b in range(nb):
        gram_out[b] = flat[b : b + 1, :]

    @pl.loop(0, G)
    def _(d):
        r = row_at(d)
        to_owners(
            r,
            offsets,
            lambda b, to: remote(gram_out.at[b], gram_in.at[w], gram_send.at[0], gram_recv.at[0], to),
            lambda b: pltpu.make_async_copy(gram_out.at[b], gram_in.at[w], gram_recv.at[0]),
        )

    @pl.loop(0, G)
    def _(r):
        send_blocks(r, near)

    arrived(gram_in, gram_recv.at[0])
    whole = jnp.sum(gram_in[...], axis=0) * (1.0 / nodes)

    entry = {}
    for a in range(VEC):
        for c in range(a + 1):
            i = a * VEC + c
            entry[a, c] = jnp.broadcast_to(whole[:, i : i + 1], (VEC, BS))
    groups = 2 * wide // VEC

    def tiles(group):
        return [recv[pl.ds(group * VEC * VEC + s, VEC, stride=VEC), :] for s in range(VEC)]

    lower, inverse = {}, []
    for j in range(VEC):
        rest = entry[j, j]
        for k in range(j):
            rest = rest - lower[j, k] * lower[j, k]
        root = lax.rsqrt(rest)
        root = root * (1.5 - 0.5 * rest * root * root)
        inverse.append(root)
        for i in range(j + 1, VEC):
            value = entry[i, j]
            for k in range(j):
                value = value - lower[i, k] * lower[j, k]
            lower[i, j] = value * root
    for a in range(VEC):
        row = {}
        for c in reversed(range(VEC)):
            value = rot_wide[c * VEC + a]
            for k in range(c + 1, VEC):
                value = value - row[k] * lower[k, c]
            row[c] = value * inverse[c]
            mixer[a * VEC + c] = row[c]

    arrived(recv, fin_recv.at[0])

    @pl.loop(0, groups)
    def _(group):
        x = tiles(group)
        for a in range(VEC):
            value = mixer[a * VEC] * x[0]
            for c in range(1, VEC):
                value = value + mixer[a * VEC + c] * x[c]
            out[a, 0, pl.ds(pl.multiple_of(group * VEC, VEC), VEC), :] = value

    for d in range(1, G):
        slab_copy(d).wait_send()
        codes_copy(d).wait_send()
    for half in range(2):
        h_copy(half, 1).wait_send()
        h_copy(half, 3).wait_send()
    h_forward(first).wait_send()
    h_forward(other).wait_send()

    @pl.loop(0, DEG)
    def _(n):
        @pl.loop(0, G)
        def _(r):
            @pl.when(has_left)
            def _():
                halo_copy(n, r, 0).wait_send()

            @pl.when(has_right)
            def _():
                halo_copy(n, r, 1).wait_send()

    @pl.when(is_own)
    def _():
        part = recv.at[pl.ds(0, (wide - 1) * 2 * VEC)]
        arrived(part, fin_send.at[0])
        part = gram_in.at[pl.ds(0, wide - 1)]
        arrived(part, gram_send.at[0])

    @pl.when(jnp.logical_not(is_own))
    def _():
        arrived(recv, fin_send.at[0])
        arrived(gram_in, gram_send.at[0])


def body(slab, hblocks, blist, rotation):
    wide = lax.axis_size("wide")
    states = slab.shape[0]
    chunk = states // G
    nb = wide // G
    nodes = G * 2 * wide * BS
    dma = pltpu.SemaphoreType.DMA
    any_space = pl.BlockSpec(memory_space=pltpu.HBM)
    operands = (slab.reshape(2 * states, BS), hblocks.reshape(2, K, BS, BS), blist, jnp.transpose(rotation, (1, 2, 0)))
    operands = [pltpu.with_memory_space_constraint(value, pltpu.HBM) for value in operands]
    return pl.pallas_call(
        functools.partial(kernel, wide, nodes),
        out_shape=jax.ShapeDtypeStruct((VEC, 1, 2 * wide, BS), F32),
        in_specs=[any_space, any_space, any_space, any_space],
        out_specs=pl.BlockSpec(memory_space=pltpu.VMEM),
        scratch_shapes=[
            pltpu.VMEM((G, 2 * chunk, BS), F32),
            pltpu.VMEM((G, 2, K, BS, BS), F32),
            pltpu.VMEM((G, 2, K), jnp.int32),
            pltpu.SMEM((G, 2, K), jnp.int32),
            pltpu.SMEM((G, 16), jnp.int32),
            pltpu.VMEM((G, 2, K * BS, 2 * BS), BF16),
            pltpu.VMEM((DEG, G, 2, chunk, BS), F32),
            pltpu.VMEM((DEG, G, 2, chunk, BS), F32),
            pltpu.VMEM((DEG, 24, 2 * chunk, BS), BF16),
            pltpu.VMEM((G, nb, 2 * VEC, BS), F32),
            pltpu.VMEM((wide * 2 * VEC, BS), F32),
            pltpu.VMEM((G, 2 * chunk, 2 * BS), BF16),
            pltpu.VMEM((2 * chunk, 2 * chunk), F32),
            pltpu.VMEM((nb, 1, BS), F32),
            pltpu.VMEM((wide, 1, BS), F32),
            pltpu.VMEM((VEC, VEC, wide), F32),
            pltpu.VMEM((VEC * VEC, VEC, BS), F32),
            pltpu.VMEM((VEC * VEC, VEC, BS), F32),
            dma((5,)),
            dma((G,)),
            dma((G,)),
            dma((G,)),
            dma((G,)),
            dma((2, 3)),
            dma((G, 2)),
            dma((DEG, G, 2)),
            dma((DEG, G, 2)),
            dma((1,)),
            dma((1,)),
            dma((1,)),
            dma((1,)),
            pltpu.SemaphoreType.REGULAR((max(1, len(reach_steps(wide))),)),
        ],
        compiler_params=pltpu.CompilerParams(
            collective_id=0, has_side_effects=True, vmem_limit_bytes=40 * 1024 * 1024
        ),
        cost_estimate=pl.CostEstimate(flops=3 * 10**9, bytes_accessed=2 * 1024 * 1024, transcendentals=0),
    )(*operands)


def solution(mesh):
    in_specs = (
        P(None, "grp", "wide", None),
        P("grp", "wide", None, None, None),
        P("grp", "wide", None),
        P(),
    )
    out_specs = P("wide", "grp", None, None)
    return jax.shard_map(body, mesh=mesh, in_specs=in_specs, out_specs=out_specs, check_vma=False)
```
